512 devices in a mesh: shot: 32 (over y, x), tm: 16 (over z, core).
Axes of the slice: x: 4, y: 8, z: 8, core: 2. Of those that a mesh axis runs over, the one named last changes fastest.
Arguments:
- records: bfloat16 [32, 64, 2048], P('shot', None, 'tm'), may hold values from -6 to 6
- live: int32 [32, 64], P('shot'), may hold values 0 or 1
- dither: int32 [32], replicated, may hold values from 0 to 32, as said below
- designature: bfloat16 [9, 33], replicated, may hold values from -0.375 to 0.375
- first_weights: bfloat16 [64, 30], replicated, may hold values from -1.5 to 1.5
- first_bias: float32 [64], replicated, may hold values from -2.5 to 2.5
- hidden_weights: bfloat16 [3, 64, 192], replicated, may hold values from -0.625 to 0.625
- hidden_bias: float32 [3, 64], replicated, may hold values from -2.5 to 2.5
- out_weights: bfloat16 [64], replicated, may hold values from -0.75 to 0.75
- out_bias: float32 [1], replicated, may hold values from -2.5 to 2.5
- shaping: bfloat16 [9, 33], replicated, may hold values from -0.375 to 0.375
Outputs:
- interference: bfloat16 [32, 64, 2048], P('shot', None, 'tm')
- cleaned: bfloat16 [32, 64, 2048], P('shot', None, 'tm')
The draws below stay inside these ranges and needn't reach their ends.
Inputs may be any that keep to these rules, and one draw needn't show every extreme that they name: One shot's dither is exactly 32 and one shot's is 0.
All inputs are finite; a program needn't handle non-finite values. No bound on the sum of `live` on one device may be relied on, other than what follows from the above.
Results may differ from the reference program's by a relative error of at most 0.012.
The reference program's roundings to bfloat16 on the way count: a program that leaves them out, or rounds other values in their place, can miss the bound.
Values may be sent and summed in bfloat16 or wider, within the bound.
A program may use at most 64 MiB of HBM per device.

```python
import jax
import jax.numpy as jnp
from jax import lax

CH = 64
HID = 3
FN = 9
FT = 33
SHOT_TAPS = 5
DMAX = 32
SHOTS = 32
NODES = 64
TIME = 2048


def draw_dither(key, part):
    first_key, second_key = jax.random.split(jax.random.fold_in(key, 7))
    values = jax.random.randint(first_key, (SHOTS,), 0, DMAX + 1)
    spot = jax.random.randint(second_key, (), 0, SHOTS)
    values = values.at[spot].set(DMAX)
    values = values.at[(spot + 1) % SHOTS].set(0)
    return values.astype(jnp.int32)


def touch_ends(values, own_key, least, top_value):
    spot = [jax.random.randint(jax.random.fold_in(own_key, axis), (), 0, length) for axis, length in enumerate(values.shape)]
    main_axis = values.shape.index(max(values.shape))
    beside = spot[:main_axis] + [(spot[main_axis] + 1) % values.shape[main_axis]] + spot[main_axis + 1:]
    return values.at[tuple(spot)].set(least).at[tuple(beside)].set(top_value)


def level_of(stream_key, dims, shards, least, top_value):
    def one(position, blocks):
        draws = jax.random.uniform(jax.random.fold_in(jax.random.fold_in(stream_key, 6), position), (blocks,), jnp.float32, least / len(shards), top_value / len(shards))
        return jnp.repeat(jnp.exp(draws), dims[position] // blocks).reshape((-1,) + (1,) * (len(dims) - position - 1))

    factor_of = one(*shards[0])
    for cut in shards[1:]:
        factor_of = factor_of * one(*cut)
    return factor_of


def gaussian(key, extent, deviation, reach, pieces=(), held_as=jnp.bfloat16):
    values = jax.random.normal(key, extent, jnp.float32) * deviation
    if len(pieces) > 0:
        values = level_of(key, extent, pieces, -0.22, 0.18) * values
    return jnp.clip(values, min=-reach, max=reach).astype(held_as)


def setup_inputs(seed: int = 0) -> dict:
    key_list = jax.random.split(jax.random.key(seed), 12)
    return {
        "records": gaussian(key_list[0], (SHOTS, NODES, TIME), 1.0, 6.0, ((0, 32), (2, 16))),
        "live": touch_ends((jax.random.randint(key_list[1], (SHOTS, NODES), 0, 4) < 3).astype(jnp.int32), jax.random.fold_in(key_list[1], 1), 0, 1),
        "dither": draw_dither(jax.random.fold_in(key_list[11], 71), 0),
        "designature": gaussian(key_list[3], (FN, FT), (FN * FT) ** -0.5, 0.375),
        "first_weights": gaussian(key_list[4], (CH, 6 * SHOT_TAPS), (3 * SHOT_TAPS) ** -0.5, 1.5),
        "first_bias": gaussian(key_list[5], (CH,), 0.5, 2.5, (), jnp.float32),
        "hidden_weights": gaussian(key_list[6], (HID, CH, 3 * CH), (3 * CH // 2) ** -0.5, 0.625),
        "hidden_bias": gaussian(key_list[7], (HID, CH), 0.5, 2.5, (), jnp.float32),
        "out_weights": gaussian(key_list[8], (CH,), CH ** -0.5, 0.75),
        "out_bias": gaussian(key_list[9], (1,), 0.5, 2.5, (), jnp.float32),
        "shaping": gaussian(key_list[10], (FN, FT), (FN * FT) ** -0.5, 0.375),
    }


def shot_filter(traces, taps):
    result = lax.conv_general_dilated(
        traces.astype(jnp.float32)[:, None], taps.astype(jnp.float32)[None, None],
        (1, 1), ((FN // 2, FN // 2), (FT // 2, FT // 2)), precision=lax.Precision.HIGHEST)
    return result[:, 0]


def reference(records, live, dither, designature, first_weights, first_bias, hidden_weights, hidden_bias, out_weights, out_bias, shaping):
    keep = live[:, :, None] > 0
    masked = jnp.where(keep, records, jnp.zeros_like(records))
    filtered = jnp.where(keep, shot_filter(masked, designature), 0.0).astype(jnp.bfloat16)

    def one_gather(gather_rows):
        padded = jnp.pad(gather_rows, ((0, 0), (0, DMAX)))
        retimed = jax.vmap(lambda row, delay: lax.dynamic_slice_in_dim(row, delay, TIME))(padded, dither)
        inputs = jnp.stack([gather_rows, retimed]).astype(jnp.float32)
        shot_pad = jnp.pad(inputs, ((0, 0), (SHOT_TAPS // 2, SHOT_TAPS // 2), (1, 1)))
        columns = jnp.stack([shot_pad[channel, offset:offset + SHOTS, shift:shift + TIME]
                             for channel in range(2) for offset in range(SHOT_TAPS) for shift in range(3)])
        summed = jnp.einsum('of,fst->ost', first_weights.astype(jnp.float32), columns) + first_bias[:, None, None]
        active = jax.nn.relu(summed).astype(jnp.bfloat16)
        for layer in range(HID):
            dilation = 2 ** (layer + 1)
            padded_act = jnp.pad(active, ((0, 0), (0, 0), (dilation, dilation)))
            stacked = jnp.concatenate([padded_act[:, :, shift * dilation:shift * dilation + TIME] for shift in range(3)], axis=0)
            summed = jnp.einsum('of,fst->ost', hidden_weights[layer].astype(jnp.float32), stacked.astype(jnp.float32))
            summed = summed + hidden_bias[layer][:, None, None]
            active = jax.nn.relu(summed).astype(jnp.bfloat16)
        result = jnp.einsum('c,cst->st', out_weights.astype(jnp.float32), active.astype(jnp.float32)) + out_bias[0]
        return result.astype(jnp.bfloat16)

    predicted = lax.map(one_gather, jnp.transpose(filtered, (1, 0, 2)))
    predicted = jnp.transpose(predicted, (1, 0, 2))
    interference = jnp.where(keep, predicted, jnp.zeros_like(predicted))
    deblended = (filtered.astype(jnp.float32) - interference.astype(jnp.float32)).astype(jnp.bfloat16)
    cleaned = jnp.where(keep, shot_filter(deblended, shaping), 0.0).astype(jnp.bfloat16)
    return interference, cleaned
```

```python
import functools

import jax
import jax.numpy as jnp
from jax import lax
from jax.experimental import pallas as pl
from jax.experimental.pallas import tpu as pltpu
from jax.sharding import PartitionSpec as P

HID = 3
FN = 9
FT = 33
SHOT_TAPS = 5
CH = 64
N = 64
L = 128
GAP = 24
GROUPS = 12
US = 8 * GROUPS
SLOT = {0: 0, -1: 1, 1: 2, -2: 3, 2: 4}
ORDER = (-1, 1, -2, 2)
MESH = pl.DeviceIdType.MESH
BF = jnp.bfloat16
F32 = jnp.float32


def iota(shape, dim):
    return lax.broadcasted_iota(jnp.int32, shape, dim)


def dot_nn(a, b):
    return jnp.dot(a, b, preferred_element_type=F32)


def dot_nt(a, b):
    return lax.dot_general(a, b, (((1,), (1,)), ((), ())), preferred_element_type=F32)


def circulants(taps, store):
    pick = iota((FT, L), 0) == ((FT // 2 - iota((FT, L), 1)) & (L - 1))
    rows = dot_nn(taps, pick.astype(BF))
    near = jnp.abs(iota((L, L), 0) - iota((L, L), 1)) <= L // 2
    for a in range(FN):
        full = jnp.broadcast_to(rows[a : a + 1, :], (L, L))
        full = pltpu.roll(full, 0, 1, stride=1, stride_axis=0)
        store(a, jnp.where(near, full, 0.0).astype(BF), jnp.where(near, 0.0, full).astype(BF))


def kernel(
    shots,
    tms,
    rec,
    live,
    dith,
    des,
    fw,
    fb,
    hw,
    hb,
    ow,
    ob,
    shp,
    inter_out,
    clean_out,
    blk,
    live_in,
    xs,
    c1,
    c2,
    w0,
    wh,
    wo,
    b0s,
    planes,
    gs,
    a0,
    a1,
    a2,
    ds,
    shot_send,
    shot_recv,
    live_send,
    live_recv,
    tm_send,
    tm_recv,
):
    s, z = lax.axis_index("shot"), lax.axis_index("tm")
    z_up, z_down = lax.rem(z + 1, tms), lax.rem(z + tms - 1, tms)

    def shot_at(offset):
        return lax.rem(s + offset + shots, shots)

    barrier = pltpu.get_barrier_semaphore()
    for offset in ORDER:
        pl.semaphore_signal(barrier, inc=1, device_id=(shot_at(offset), z), device_id_type=MESH)
    for other in (z_up, z_down):
        pl.semaphore_signal(barrier, inc=1, device_id=(s, other), device_id_type=MESH)
    pl.semaphore_wait(barrier, 6)

    def send(src, dst, send_sem, recv_sem, device):
        copy = pltpu.make_async_remote_copy(
            src_ref=src, dst_ref=dst, send_sem=send_sem, recv_sem=recv_sem,
            device_id=device, device_id_type=MESH,
        )
        copy.start()
        return copy

    shot_copies, live_copies, tm_copies = {}, {}, []

    def forward(slot, source):
        for side, other in ((0, z_up), (1, z_down)):
            tm_copies.append(
                send(source, blk.at[slot, side], tm_send.at[slot, side], tm_recv.at[slot, side], (s, other))
            )

    for offset in ORDER:
        slot = SLOT[-offset]
        target = (shot_at(offset), z)
        shot_copies[-offset] = send(rec, blk.at[slot, 2], shot_send.at[slot], shot_recv.at[slot], target)
        live_copies[-offset] = send(live, live_in.at[slot], live_send.at[slot], live_recv.at[slot], target)
    forward(0, rec)

    def keep_first(a, near, far):
        c1[a, 0:L, 0:L] = near
        c1[a, 0:L, L:] = far
        c1[a, L:, 0:L] = far
        c1[a, L:, L:] = near

    circulants(des[...], keep_first)

    for offset in ORDER:
        shot_copies[offset].wait_recv()
        forward(SLOT[offset], blk.at[SLOT[offset], 2])

    def keep_second(a, near, far):
        c2[a, 0:L, :] = near
        c2[a, L:, :] = far

    circulants(shp[...], keep_second)

    lane = iota((1, L), 1)
    upper = lane >= CH
    row, col = iota((256, 32), 0), iota((256, 32), 1)
    third = lax.shift_right_logical(col * 43, 7)
    place = (row == GAP * third + (col - 3 * third)) & (col < 6 * SHOT_TAPS)
    first = fw[...]
    doubled = jnp.concatenate([first, first], axis=0)
    b0s[0:16, :] = jnp.zeros((16, L), F32)
    b0s[16:, :] = dot_nt(place.astype(BF)[:, : 6 * SHOT_TAPS], doubled)
    for pair in range(8):
        even, odd = b0s[pl.ds(16 - 2 * pair, 256), :], b0s[pl.ds(15 - 2 * pair, 256), :]
        w0[:, pair * L : (pair + 1) * L] = jnp.where(upper, odd, even).astype(BF)

    same_half = (iota((L, L), 0) >= CH) == (iota((L, L), 1) >= CH)
    zero_block = jnp.zeros((L, L), BF)
    for layer in range(HID):
        weights = hw[layer]
        doubled = jnp.concatenate([weights, weights], axis=0)
        wh[layer, 3 * L :, 0:L] = zero_block
        wh[layer, 0:L, L:] = zero_block
        for k in range(3):
            pick = iota((L, 3 * CH), 1) == (k * CH + (iota((L, 3 * CH), 0) & (CH - 1)))
            block = jnp.where(same_half, dot_nt(pick.astype(BF), doubled), 0.0).astype(BF)
            wh[layer, k * L : (k + 1) * L, 0:L] = block
            wh[layer, (k + 1) * L : (k + 2) * L, L:] = block

    pick = iota((L, CH), 1) == (iota((L, CH), 0) & (CH - 1))
    spread = dot_nt(pick.astype(BF), jnp.broadcast_to(ow[...], (L, CH)))
    for r in range(4):
        for i in range(2):
            step = 8 * i + 2 * r
            here = (iota((L, L), 1) & 15) == step + jnp.where(iota((L, L), 0) >= CH, 1, 0)
            wo[(2 * r + i) * L : (2 * r + i + 1) * L, :] = jnp.where(here, spread, 0.0).astype(BF)

    def wide(bias):
        both = jnp.concatenate([bias, bias], axis=1)
        return jnp.concatenate([both, both], axis=1)

    first_bias = wide(fb[...])
    hidden_bias = [wide(hb[layer : layer + 1, :]) for layer in range(HID)]

    has_left, has_right = z > 0, z < tms - 1
    left_f, right_f = jnp.where(has_left, 1.0, 0.0), jnp.where(has_right, 1.0, 0.0)
    halo = jnp.where(lane < 80, right_f, left_f)
    time_ok = jnp.concatenate([jnp.ones((1, L), F32), halo], axis=1)
    diagonal = iota((N, N), 0) == iota((N, N), 1)

    def live_column(offset):
        values = live[...] if offset == 0 else live_in[SLOT[offset]]
        there = (s + offset >= 0) & (s + offset < shots)
        values = jnp.where(there, values, 0).astype(F32)
        spread_rows = jnp.where(diagonal, jnp.broadcast_to(values, (N, N)), 0.0)
        return jnp.sum(spread_rows, axis=1, keepdims=True)

    kept = {}

    def fill(offset):
        slot = SLOT[offset]
        column = live_column(offset)
        kept[offset] = (column * time_ok) > 0.0
        centre = rec[...] if offset == 0 else blk[slot, 2]
        sides = jnp.where(lane < 80, blk[slot, 1].astype(F32), blk[slot, 0].astype(F32))
        xs[slot, 0:8, :] = jnp.zeros((8, 2 * L), F32)
        xs[slot, 72:80, :] = jnp.zeros((8, 2 * L), F32)
        xs[slot, 8:72, 0:L] = jnp.where(column > 0.0, centre.astype(F32), 0.0)
        xs[slot, 8:72, L:] = jnp.where((column * halo) > 0.0, sides, 0.0)

    def filtered(offsets):
        total = None
        for a in range(FN):
            rows = [xs[SLOT[o], pl.ds(4 + a, N), :] for o in offsets]
            left = jnp.concatenate(rows, axis=0).astype(BF)
            term = dot_nn(left, c1[a])
            total = term if total is None else total + term
        return {o: jnp.where(kept[o], total[i * N : (i + 1) * N], 0.0).astype(BF).astype(F32)
                for i, o in enumerate(offsets)}

    lanes2 = iota((1, 2 * L), 1)

    def make_planes(offset, values):
        a = offset + SHOT_TAPS // 2
        planes[a] = pltpu.roll(values, GAP * a + 33, 1).astype(BF)
        p = a + SHOT_TAPS
        delay = dith[shot_at(offset)]
        moved = pltpu.roll(values, GAP * p + 33 - delay, 1)
        early = (lanes2 >= GAP * p) & (lanes2 < GAP * p + 33)
        planes[p] = jnp.where(jnp.where(early, left_f, 1.0) > 0.0, moved, 0.0).astype(BF)

    own = None
    for offsets in ((0, -1, 1), (-2, 2)):
        for offset in offsets:
            slot = SLOT[offset]
            if offset != 0:
                live_copies[offset].wait_recv()
            for copy in tm_copies[2 * slot : 2 * slot + 2]:
                copy.wait_recv()
            fill(offset)
        done = filtered(offsets)
        for offset in offsets:
            make_planes(offset, done[offset])
        if 0 in done:
            own = done[0]

    for part in range(2):
        rows = slice(part * 32, part * 32 + 32)
        held = [planes[p, rows, :].astype(F32) for p in range(2 * SHOT_TAPS)]
        for g in range(GROUPS):
            place = (lanes2 - 16 * g) & 255
            merged = held[0]
            for p in range(1, 2 * SHOT_TAPS):
                merged = jnp.where(place >= GAP * p, held[p], merged)
            if g:
                merged = pltpu.roll(merged, 256 - 16 * g, 1)
            gs[g, rows, :] = merged.astype(BF)

    def finish(total, bias, factor):
        act = jnp.maximum(total + bias, 0.0)
        if factor is not None:
            act = act * factor
        return act.astype(BF)

    for g0, g1, factor in ((0, 2, left_f), (2, 6, None), (6, 10, None), (10, 12, right_f)):
        left = gs[g0:g1].reshape((g1 - g0) * N, 256)
        for quarter in range(4):
            act = finish(dot_nn(left, w0[:, quarter * 256 : (quarter + 1) * 256]), first_bias, factor)
            for g in range(g0, g1):
                for i in range(2):
                    at = (g - g0) * N
                    a0[8 * g + 2 * quarter + i] = act[at : at + N, i * L : (i + 1) * L]

    def chunks(lo, hi, size):
        cuts = [lo, 16 // size, 80 // size, hi]
        return [(cuts[0], cuts[1], left_f), (cuts[1], cuts[2], None), (cuts[2], cuts[3], right_f)]

    def layer(source, target, index, lo, hi, most):
        step = 1 << index
        for start, stop, factor in chunks(lo, hi, 2 * step):
            for j0 in range(start, stop, most):
                js = range(j0, min(j0 + most, stop))
                us = [2 * step * j + r for j in js for r in range(step)]
                left = jnp.concatenate(
                    [jnp.concatenate([source[u - step], source[u], source[u + step], source[u + 2 * step]], axis=1)
                     for u in us], axis=0)
                act = finish(dot_nn(left, wh[index]), hidden_bias[index], factor)
                target(us, step, act)

    def into(ref):
        def keep(us, step, act):
            for m, u in enumerate(us):
                ref[u] = act[m * N : (m + 1) * N, 0:L]
                ref[u + step] = act[m * N : (m + 1) * N, L:]
        return keep

    column = live_column(0)
    alive = column > 0.0
    out_bias = ob[0]
    sixteen = lax.shift_right_logical(lane, 4)
    pred = {}

    def finish_pred(us, step, act):
        for q in range(len(us) // step):
            left = jnp.concatenate(
                [act[(q * step + r) * N : (q * step + r + 1) * N] for r in range(step)], axis=1)
            pred[us[q * step] // 8] = (dot_nn(left, wo[...]) + out_bias).astype(BF).astype(F32)

    layer(a0, into(a1), 0, 1, 47, 8)
    layer(a1, into(a2), 1, 1, 23, 4)
    layer(a2, finish_pred, 2, 1, 11, 2)

    middle = pred[2]
    for j in range(3, 10):
        middle = jnp.where(sixteen == j - 2, pred[j], middle)
    middle = jnp.where(alive, middle, 0.0)
    inter_out[...] = middle.astype(BF)
    edge = jnp.where(lane < 80, pred[10], pred[1])
    edge = jnp.where((column * halo) > 0.0, edge, 0.0)
    rest = (own - jnp.concatenate([middle, edge], axis=1)).astype(BF).astype(F32)
    ds[0:8, :] = jnp.zeros((8, 2 * L), F32)
    ds[72:80, :] = jnp.zeros((8, 2 * L), F32)
    ds[8:72, :] = rest
    total = None
    for a in range(FN):
        term = dot_nn(ds[pl.ds(4 + a, N), :].astype(BF), c2[a])
        total = term if total is None else total + term
    clean_out[...] = jnp.where(alive, total, 0.0).astype(BF)

    for copy in list(shot_copies.values()) + list(live_copies.values()) + tm_copies:
        copy.wait_send()


def local(shots, tms, records, live, dither, designature, first_weights, first_bias, hidden_weights, hidden_bias,
          out_weights, out_bias, shaping):
    vmem = pl.BlockSpec(memory_space=pltpu.VMEM)
    smem = pl.BlockSpec(memory_space=pltpu.SMEM)
    shape = jax.ShapeDtypeStruct((N, L), BF)
    inter, clean = pl.pallas_call(
        functools.partial(kernel, shots, tms),
        out_shape=(shape, shape),
        in_specs=[vmem, vmem, smem, vmem, vmem, vmem, vmem, vmem, vmem, smem, vmem],
        out_specs=(vmem, vmem),
        scratch_shapes=[
            pltpu.VMEM((5, 3, N, L), BF),
            pltpu.VMEM((5, 1, N), jnp.int32),
            pltpu.VMEM((5, 80, 2 * L), F32),
            pltpu.VMEM((FN, 2 * L, 2 * L), BF),
            pltpu.VMEM((FN, 2 * L, L), BF),
            pltpu.VMEM((256, 1024), BF),
            pltpu.VMEM((HID, 4 * L, 2 * L), BF),
            pltpu.VMEM((1024, L), BF),
            pltpu.VMEM((272, L), F32),
            pltpu.VMEM((2 * SHOT_TAPS, N, 2 * L), BF),
            pltpu.VMEM((GROUPS, N, 2 * L), BF),
            pltpu.VMEM((US, N, L), BF),
            pltpu.VMEM((US, N, L), BF),
            pltpu.VMEM((US, N, L), BF),
            pltpu.VMEM((80, 2 * L), F32),
            pltpu.SemaphoreType.DMA((5,)),
            pltpu.SemaphoreType.DMA((5,)),
            pltpu.SemaphoreType.DMA((5,)),
            pltpu.SemaphoreType.DMA((5,)),
            pltpu.SemaphoreType.DMA((5, 2)),
            pltpu.SemaphoreType.DMA((5, 2)),
        ],
        compiler_params=pltpu.CompilerParams(
            collective_id=0, has_side_effects=True, vmem_limit_bytes=48 * 1024 * 1024
        ),
    )(
        records.reshape(N, L),
        live,
        dither,
        designature,
        first_weights,
        first_bias.reshape(1, CH),
        hidden_weights,
        hidden_bias,
        out_weights.reshape(1, CH),
        out_bias,
        shaping,
    )
    return inter.reshape(1, N, L), clean.reshape(1, N, L)


def solution(mesh):
    shots, tms = mesh.shape["shot"], mesh.shape["tm"]
    in_specs = (P("shot", None, "tm"), P("shot", None), P(), P(), P(), P(), P(), P(), P(), P(), P())
    out_specs = (P("shot", None, "tm"), P("shot", None, "tm"))
    return jax.shard_map(
        functools.partial(local, shots, tms), mesh=mesh, in_specs=in_specs, out_specs=out_specs, check_vma=False
    )
```

```python
import functools

import jax
import jax.numpy as jnp
from jax import lax
from jax.experimental import pallas as pl
from jax.experimental.pallas import tpu as pltpu
from jax.sharding import PartitionSpec as P

HID = 3
FN = 9
FT = 33
SHOT_TAPS = 5
CH = 64
N = 64
L = 128
GAP = 24
GROUPS = 12
US = 8 * GROUPS
SLOT = {0: 0, -1: 1, 1: 2, -2: 3, 2: 4}
MESH = pl.DeviceIdType.MESH
BF = jnp.bfloat16
F32 = jnp.float32


def iota(shape, dim):
    return lax.broadcasted_iota(jnp.int32, shape, dim)


def dot_nn(a, b):
    return jnp.dot(a, b, preferred_element_type=F32)


def dot_nt(a, b):
    return lax.dot_general(a, b, (((1,), (1,)), ((), ())), preferred_element_type=F32)


def circulants(taps, store):
    pick = iota((FT, L), 0) == ((FT // 2 - iota((FT, L), 1)) & (L - 1))
    rows = dot_nn(taps, pick.astype(BF))
    near = jnp.abs(iota((L, L), 0) - iota((L, L), 1)) <= L // 2
    for a in range(FN):
        full = jnp.broadcast_to(rows[a : a + 1, :], (L, L))
        full = pltpu.roll(full, 0, 1, stride=1, stride_axis=0)
        store(a, jnp.where(near, full, 0.0).astype(BF), jnp.where(near, 0.0, full).astype(BF))


def kernel(
    shots,
    tms,
    rec_hbm,
    live_hbm,
    dith_hbm,
    des_hbm,
    fw_hbm,
    fb_hbm,
    hw_hbm,
    hb_hbm,
    ow_hbm,
    ob_hbm,
    shp_hbm,
    inter_out,
    clean_out,
    rec,
    live,
    dith,
    des,
    fw,
    fb,
    hw,
    hb,
    ow,
    ob,
    shp,
    halos,
    win,
    xs,
    c1,
    c2,
    w0,
    wh,
    wo,
    b0s,
    planes,
    gs,
    a0,
    a1,
    a2,
    ds,
    in_sem,
    tm_send,
    tm_recv,
    shot_send,
    shot_recv,
):
    s, z = lax.axis_index("shot"), lax.axis_index("tm")
    has_left, has_right = z > 0, z < tms - 1
    has_before, has_after = s > 0, s < shots - 1
    has_before2, has_after2 = s > 1, s < shots - 2

    barrier = pltpu.get_barrier_semaphore()
    expected = 0
    for here, device in (
        (has_left, (s, z - 1)),
        (has_right, (s, z + 1)),
        (has_before, (s - 1, z)),
        (has_after, (s + 1, z)),
    ):
        @pl.when(here)
        def _(device=device):
            pl.semaphore_signal(barrier, inc=1, device_id=device, device_id_type=MESH)
        expected = expected + here.astype(jnp.int32)

    fetches = [
        pltpu.make_async_copy(src, dst, in_sem.at[i])
        for i, (src, dst) in enumerate((
            (des_hbm, des), (rec_hbm, rec), (live_hbm, live), (fw_hbm, fw), (hw_hbm, hw), (dith_hbm, dith),
            (ow_hbm, ow), (shp_hbm, shp), (fb_hbm, fb), (hb_hbm, hb), (ob_hbm, ob)))
    ]
    for fetch in fetches:
        fetch.start()

    def remote(src, dst, send_sem, recv_sem, device):
        return pltpu.make_async_remote_copy(
            src_ref=src, dst_ref=dst, send_sem=send_sem, recv_sem=recv_sem,
            device_id=device, device_id_type=MESH,
        )

    to_right = remote(rec_hbm, halos.at[0], tm_send.at[0], tm_recv.at[0], (s, z + 1))
    to_left = remote(rec_hbm, halos.at[1], tm_send.at[1], tm_recv.at[1], (s, z - 1))

    def to_shot(index, source, target, device):
        return remote(win.at[SLOT[source]], win.at[SLOT[target]], shot_send.at[index], shot_recv.at[index], device)

    to_after = to_shot(0, 0, -1, (s + 1, z))
    to_before = to_shot(1, 0, 1, (s - 1, z))
    on_after = to_shot(2, -1, -2, (s + 1, z))
    on_before = to_shot(3, 1, 2, (s - 1, z))

    def keep_first(a, near, far):
        c1[a, 0:L, 0:L] = near
        c1[a, 0:L, L:] = far
        c1[a, L:, 0:L] = far
        c1[a, L:, L:] = near

    fetches[0].wait()
    circulants(des[...], keep_first)

    pl.semaphore_wait(barrier, expected)

    @pl.when(has_right)
    def _():
        to_right.start()

    @pl.when(has_left)
    def _():
        to_left.start()

    for fetch in fetches[1:]:
        fetch.wait()

    lane = iota((1, L), 1)
    left_f, right_f = jnp.where(has_left, 1.0, 0.0), jnp.where(has_right, 1.0, 0.0)
    halo = jnp.where(lane < 80, right_f, left_f)
    time_ok = jnp.concatenate([jnp.ones((1, L), F32), halo], axis=1)
    diagonal = iota((N, N), 0) == iota((N, N), 1)
    spread_rows = jnp.where(diagonal, jnp.broadcast_to(live[...].astype(F32), (N, N)), 0.0)
    column = jnp.sum(spread_rows, axis=1, keepdims=True)
    alive = column > 0.0
    alive_halo = (column * halo) > 0.0

    xs[0:8, :] = jnp.zeros((8, 2 * L), F32)
    xs[72:80, :] = jnp.zeros((8, 2 * L), F32)
    xs[8:72, 0:L] = jnp.where(alive, rec[...].astype(F32), 0.0)

    upper = lane >= CH
    row, col = iota((256, 6 * SHOT_TAPS), 0), iota((256, 6 * SHOT_TAPS), 1)
    third = lax.shift_right_logical(col * 43, 7)
    place = row == GAP * third + (col - 3 * third)
    base = dot_nn(place.astype(BF), fw[...])
    b0s[0:16, :] = jnp.zeros((16, L), F32)
    b0s[16:, :] = jnp.concatenate([base, base], axis=1)
    for pair in range(8):
        even, odd = b0s[pl.ds(16 - 2 * pair, 256), :], b0s[pl.ds(15 - 2 * pair, 256), :]
        w0[:, pair * L : (pair + 1) * L] = jnp.where(upper, odd, even).astype(BF)

    @pl.when(has_left)
    def _():
        to_right.wait_recv()

    @pl.when(has_right)
    def _():
        to_left.wait_recv()

    sides = jnp.where(lane < 80, halos[1].astype(F32), halos[0].astype(F32))
    xs[8:72, L:] = jnp.where(alive_halo, sides, 0.0)

    def filter_with(source, matrices):
        total = None
        for a in range(FN):
            term = dot_nn(source[pl.ds(4 + a, N), :].astype(BF), matrices[a])
            total = term if total is None else total + term
        return total

    win[0] = jnp.where((column * time_ok) > 0.0, filter_with(xs, c1), 0.0).astype(BF)

    @pl.when(has_after)
    def _():
        to_after.start()

    @pl.when(has_before)
    def _():
        to_before.start()

    lanes2 = iota((1, 2 * L), 1)

    def make_planes(offset, there):
        values = win[SLOT[offset]].astype(F32)
        if there is not None:
            values = jnp.where(there, values, 0.0)
        a = offset + SHOT_TAPS // 2
        planes[a] = pltpu.roll(values, GAP * a + 33, 1).astype(BF)
        p = a + SHOT_TAPS
        delay = dith[lax.rem(s + offset + shots, shots)]
        moved = pltpu.roll(values, GAP * p + 33 - delay, 1)
        early = (lanes2 >= GAP * p) & (lanes2 < GAP * p + 33)
        planes[p] = jnp.where(jnp.where(early, left_f, 1.0) > 0.0, moved, 0.0).astype(BF)

    same_half = (iota((L, L), 0) >= CH) == (iota((L, L), 1) >= CH)
    zero_block = jnp.zeros((L, L), BF)
    for layer in range(HID):
        weights = hw[layer]
        doubled = jnp.concatenate([weights, weights], axis=0)
        wh[layer, 3 * L :, 0:L] = zero_block
        wh[layer, 0:L, L:] = zero_block
        for k in range(3):
            pick = iota((L, 3 * CH), 1) == (k * CH + (iota((L, 3 * CH), 0) & (CH - 1)))
            block = jnp.where(same_half, dot_nt(pick.astype(BF), doubled), 0.0).astype(BF)
            wh[layer, k * L : (k + 1) * L, 0:L] = block
            wh[layer, (k + 1) * L : (k + 2) * L, L:] = block

    pick = iota((L, CH), 1) == (iota((L, CH), 0) & (CH - 1))
    spread = dot_nt(pick.astype(BF), jnp.broadcast_to(ow[...], (L, CH)))
    for r in range(4):
        for i in range(2):
            step = 8 * i + 2 * r
            here = (iota((L, L), 1) & 15) == step + jnp.where(iota((L, L), 0) >= CH, 1, 0)
            wo[(2 * r + i) * L : (2 * r + i + 1) * L, :] = jnp.where(here, spread, 0.0).astype(BF)

    def wide(bias):
        both = jnp.concatenate([bias, bias], axis=1)
        return jnp.concatenate([both, both], axis=1)

    first_bias = wide(fb[...])
    hidden_bias = [wide(hb[layer : layer + 1, :]) for layer in range(HID)]
    make_planes(0, None)

    @pl.when(has_before)
    def _():
        to_after.wait_recv()

    @pl.when(has_before & has_after)
    def _():
        on_after.start()

    @pl.when(has_after)
    def _():
        to_before.wait_recv()

    @pl.when(has_before & has_after)
    def _():
        on_before.start()

    def keep_second(a, near, far):
        c2[a, 0:L, :] = near
        c2[a, L:, :] = far

    circulants(shp[...], keep_second)
    make_planes(-1, has_before)
    make_planes(1, has_after)

    @pl.when(has_before2)
    def _():
        on_after.wait_recv()

    @pl.when(has_after2)
    def _():
        on_before.wait_recv()

    make_planes(-2, has_before2)
    make_planes(2, has_after2)

    for part in range(2):
        rows = slice(part * 32, part * 32 + 32)
        held = [planes[p, rows, :].astype(F32) for p in range(2 * SHOT_TAPS)]
        for g in range(GROUPS):
            place = (lanes2 - 16 * g) & 255
            merged = held[0]
            for p in range(1, 2 * SHOT_TAPS):
                merged = jnp.where(place >= GAP * p, held[p], merged)
            if g:
                merged = pltpu.roll(merged, 256 - 16 * g, 1)
            gs[g, rows, :] = merged.astype(BF)

    def finish(total, bias, factor):
        act = jnp.maximum(total + bias, 0.0)
        if factor is not None:
            act = act * factor
        return act.astype(BF)

    for g0, g1, factor in ((0, 2, left_f), (2, 6, None), (6, 10, None), (10, 12, right_f)):
        left = gs[g0:g1].reshape((g1 - g0) * N, 256)
        for quarter in range(4):
            act = finish(dot_nn(left, w0[:, quarter * 256 : (quarter + 1) * 256]), first_bias, factor)
            for g in range(g0, g1):
                for i in range(2):
                    at = (g - g0) * N
                    a0[8 * g + 2 * quarter + i] = act[at : at + N, i * L : (i + 1) * L]

    def chunks(lo, hi, size):
        cuts = [lo, 16 // size, 80 // size, hi]
        return [(cuts[0], cuts[1], left_f), (cuts[1], cuts[2], None), (cuts[2], cuts[3], right_f)]

    def layer(source, target, index, lo, hi, most):
        step = 1 << index
        for start, stop, factor in chunks(lo, hi, 2 * step):
            for j0 in range(start, stop, most):
                js = range(j0, min(j0 + most, stop))
                us = [2 * step * j + r for j in js for r in range(step)]
                left = jnp.concatenate(
                    [jnp.concatenate([source[u - step], source[u], source[u + step], source[u + 2 * step]], axis=1)
                     for u in us], axis=0)
                act = finish(dot_nn(left, wh[index]), hidden_bias[index], factor)
                target(us, step, act)

    def into(ref):
        def keep(us, step, act):
            for m, u in enumerate(us):
                ref[u] = act[m * N : (m + 1) * N, 0:L]
                ref[u + step] = act[m * N : (m + 1) * N, L:]
        return keep

    out_bias = ob[0]
    sixteen = lax.shift_right_logical(lane, 4)
    pred = {}

    def finish_pred(us, step, act):
        for q in range(len(us) // step):
            left = jnp.concatenate(
                [act[(q * step + r) * N : (q * step + r + 1) * N] for r in range(step)], axis=1)
            pred[us[q * step] // 8] = (dot_nn(left, wo[...]) + out_bias).astype(BF).astype(F32)

    layer(a0, into(a1), 0, 1, 47, 8)
    layer(a1, into(a2), 1, 1, 23, 4)
    layer(a2, finish_pred, 2, 1, 11, 2)

    middle = pred[2]
    for j in range(3, 10):
        middle = jnp.where(sixteen == j - 2, pred[j], middle)
    middle = jnp.where(alive, middle, 0.0)
    inter_out[...] = middle.astype(BF)
    edge = jnp.where(lane < 80, pred[10], pred[1])
    edge = jnp.where(alive_halo, edge, 0.0)
    rest = (win[0].astype(F32) - jnp.concatenate([middle, edge], axis=1)).astype(BF).astype(F32)
    ds[0:8, :] = jnp.zeros((8, 2 * L), F32)
    ds[72:80, :] = jnp.zeros((8, 2 * L), F32)
    ds[8:72, :] = rest
    clean_out[...] = jnp.where(alive, filter_with(ds, c2), 0.0).astype(BF)

    for here, copy in (
        (has_right, to_right),
        (has_left, to_left),
        (has_after, to_after),
        (has_before, to_before),
        (has_before & has_after, on_after),
        (has_before & has_after, on_before),
    ):
        @pl.when(here)
        def _(copy=copy):
            copy.wait_send()


def local(shots, tms, records, live, dither, designature, first_weights, first_bias, hidden_weights, hidden_bias,
          out_weights, out_bias, shaping):
    vmem = pl.BlockSpec(memory_space=pltpu.VMEM)
    hbm = pl.BlockSpec(memory_space=pltpu.HBM)
    shape = jax.ShapeDtypeStruct((N, L), BF)
    inputs = (
        records.reshape(N, L),
        live,
        dither,
        designature,
        first_weights.T,
        first_bias.reshape(1, CH),
        hidden_weights,
        hidden_bias,
        out_weights.reshape(1, CH),
        out_bias,
        shaping,
    )
    spaces = [pltpu.SMEM if i in (2, 9) else pltpu.VMEM for i in range(len(inputs))]
    inter, clean = pl.pallas_call(
        functools.partial(kernel, shots, tms),
        out_shape=(shape, shape),
        in_specs=[hbm] * len(inputs),
        out_specs=(vmem, vmem),
        scratch_shapes=[
            *[space(x.shape, x.dtype) for space, x in zip(spaces, inputs)],
            pltpu.VMEM((2, N, L), BF),
            pltpu.VMEM((5, N, 2 * L), BF),
            pltpu.VMEM((80, 2 * L), F32),
            pltpu.VMEM((FN, 2 * L, 2 * L), BF),
            pltpu.VMEM((FN, 2 * L, L), BF),
            pltpu.VMEM((256, 1024), BF),
            pltpu.VMEM((HID, 4 * L, 2 * L), BF),
            pltpu.VMEM((1024, L), BF),
            pltpu.VMEM((272, L), F32),
            pltpu.VMEM((2 * SHOT_TAPS, N, 2 * L), BF),
            pltpu.VMEM((GROUPS, N, 2 * L), BF),
            pltpu.VMEM((US, N, L), BF),
            pltpu.VMEM((US, N, L), BF),
            pltpu.VMEM((US, N, L), BF),
            pltpu.VMEM((80, 2 * L), F32),
            pltpu.SemaphoreType.DMA((len(inputs),)),
            pltpu.SemaphoreType.DMA((2,)),
            pltpu.SemaphoreType.DMA((2,)),
            pltpu.SemaphoreType.DMA((4,)),
            pltpu.SemaphoreType.DMA((4,)),
        ],
        compiler_params=pltpu.CompilerParams(
            collective_id=0, has_side_effects=True, vmem_limit_bytes=61 * 1024 * 1024
        ),
    )(*inputs)
    return inter.reshape(1, N, L), clean.reshape(1, N, L)


def solution(mesh):
    shots, tms = mesh.shape["shot"], mesh.shape["tm"]
    in_specs = (P("shot", None, "tm"), P("shot", None), P(), P(), P(), P(), P(), P(), P(), P(), P())
    out_specs = (P("shot", None, "tm"), P("shot", None, "tm"))
    return jax.shard_map(
        functools.partial(local, shots, tms), mesh=mesh, in_specs=in_specs, out_specs=out_specs, check_vma=False
    )
```

```python
import functools

import jax
import jax.numpy as jnp
from jax import lax
from jax.experimental import pallas as pl
from jax.experimental.pallas import tpu as pltpu
from jax.sharding import PartitionSpec as P

HID = 3
FN = 9
FT = 33
SHOT_TAPS = 5
CH = 64
N = 64
L = 128
GAP = 24
GROUPS = 12
US = 8 * GROUPS
SLOT = {0: 0, -1: 1, 1: 2, -2: 3, 2: 4}
MESH = pl.DeviceIdType.MESH
BF = jnp.bfloat16
F32 = jnp.float32


def iota(shape, dim):
    return lax.broadcasted_iota(jnp.int32, shape, dim)


def dot_nn(a, b):
    return jnp.dot(a, b, preferred_element_type=F32)


def dot_nt(a, b):
    return lax.dot_general(a, b, (((1,), (1,)), ((), ())), preferred_element_type=F32)


def circulants(taps, store):
    pick = iota((FT, L), 0) == ((FT // 2 - iota((FT, L), 1)) & (L - 1))
    rows = dot_nn(taps, pick.astype(BF))
    near = jnp.abs(iota((L, L), 0) - iota((L, L), 1)) <= L // 2
    for a in range(FN):
        full = jnp.broadcast_to(rows[a : a + 1, :], (L, L))
        full = pltpu.roll(full, 0, 1, stride=1, stride_axis=0)
        store(a, jnp.where(near, full, 0.0).astype(BF), jnp.where(near, 0.0, full).astype(BF))


def kernel(
    shots,
    tms,
    rec_hbm,
    live_hbm,
    dith_hbm,
    des_hbm,
    fw_hbm,
    fb_hbm,
    hw_hbm,
    hb_hbm,
    ow_hbm,
    ob_hbm,
    shp_hbm,
    out,
    rec,
    live,
    dith,
    des,
    fw,
    fb,
    hw,
    hb,
    ow,
    ob,
    shp,
    halos,
    win,
    xs,
    c1,
    c2,
    w0,
    wh,
    wo,
    b0s,
    planes,
    gs,
    a0,
    a1,
    a2,
    a3,
    ds,
    in_sem,
    tm_send,
    tm_recv,
    shot_send,
    shot_recv,
):
    s, z = lax.axis_index("shot"), lax.axis_index("tm")
    has_left, has_right = z > 0, z < tms - 1
    has_before, has_after = s > 0, s < shots - 1
    has_before2, has_after2 = s > 1, s < shots - 2

    barrier = pltpu.get_barrier_semaphore()
    expected = 0
    for here, device in (
        (has_left, (s, z - 1)),
        (has_right, (s, z + 1)),
        (has_before, (s - 1, z)),
        (has_after, (s + 1, z)),
        (has_before2, (s - 2, z)),
        (has_after2, (s + 2, z)),
    ):
        @pl.when(here)
        def _(device=device):
            pl.semaphore_signal(barrier, inc=1, device_id=device, device_id_type=MESH)
        expected = expected + here.astype(jnp.int32)

    fetches = [
        pltpu.make_async_copy(src, dst, in_sem.at[i])
        for i, (src, dst) in enumerate((
            (des_hbm, des), (rec_hbm, rec), (live_hbm, live), (fw_hbm, fw), (hw_hbm, hw), (dith_hbm, dith),
            (ow_hbm, ow), (shp_hbm, shp), (fb_hbm, fb), (hb_hbm, hb), (ob_hbm, ob)))
    ]
    for fetch in fetches:
        fetch.start()

    def remote(src, dst, send_sem, recv_sem, device):
        return pltpu.make_async_remote_copy(
            src_ref=src, dst_ref=dst, send_sem=send_sem, recv_sem=recv_sem,
            device_id=device, device_id_type=MESH,
        )

    to_right = remote(rec_hbm, halos.at[0], tm_send.at[0], tm_recv.at[0], (s, z + 1))
    to_left = remote(rec_hbm, halos.at[1], tm_send.at[1], tm_recv.at[1], (s, z - 1))

    def to_shot(index, offset):
        return remote(
            win.at[0], win.at[SLOT[-offset]], shot_send.at[index], shot_recv.at[index], (s + offset, z))

    shot_copies = [
        (to_shot(i, offset), there, behind)
        for i, (offset, there, behind) in enumerate((
            (2, has_after2, has_before2),
            (-2, has_before2, has_after2),
            (1, has_after, has_before),
            (-1, has_before, has_after)))
    ]

    def keep_first(a, near, far):
        c1[a, 0:L, 0:L] = near
        c1[a, 0:L, L:] = far
        c1[a, L:, 0:L] = far
        c1[a, L:, L:] = near

    fetches[0].wait()
    circulants(des[...], keep_first)

    pl.semaphore_wait(barrier, expected)

    @pl.when(has_right)
    def _():
        to_right.start()

    @pl.when(has_left)
    def _():
        to_left.start()

    for fetch in fetches[1:]:
        fetch.wait()

    lane = iota((1, L), 1)
    left_f, right_f = jnp.where(has_left, 1.0, 0.0), jnp.where(has_right, 1.0, 0.0)
    halo = jnp.where(lane < 80, right_f, left_f)
    time_ok = jnp.concatenate([jnp.ones((1, L), F32), halo], axis=1)
    diagonal = iota((N, N), 0) == iota((N, N), 1)
    spread_rows = jnp.where(diagonal, jnp.broadcast_to(live[...].astype(F32), (N, N)), 0.0)
    column = jnp.sum(spread_rows, axis=1, keepdims=True)
    alive = column > 0.0
    alive_halo = (column * halo) > 0.0

    xs[0:8, :] = jnp.zeros((8, 2 * L), F32)
    xs[72:80, :] = jnp.zeros((8, 2 * L), F32)
    xs[8:72, 0:L] = jnp.where(alive, rec[...].astype(F32), 0.0)

    upper = lane >= CH
    row, col = iota((256, 6 * SHOT_TAPS), 0), iota((256, 6 * SHOT_TAPS), 1)
    third = lax.shift_right_logical(col * 43, 7)
    place = row == GAP * third + (col - 3 * third)
    base = dot_nn(place.astype(BF), fw[...])
    b0s[0:16, :] = jnp.zeros((16, L), F32)
    b0s[16:, :] = jnp.concatenate([base, base], axis=1)
    for pair in range(8):
        even, odd = b0s[pl.ds(16 - 2 * pair, 256), :], b0s[pl.ds(15 - 2 * pair, 256), :]
        w0[:, pair * L : (pair + 1) * L] = jnp.where(upper, odd, even).astype(BF)

    @pl.when(has_left)
    def _():
        to_right.wait_recv()

    @pl.when(has_right)
    def _():
        to_left.wait_recv()

    sides = jnp.where(lane < 80, halos[1].astype(F32), halos[0].astype(F32))
    xs[8:72, L:] = jnp.where(alive_halo, sides, 0.0)

    def filter_with(source, matrices):
        total = None
        for a in range(FN):
            term = dot_nn(source[pl.ds(4 + a, N), :].astype(BF), matrices[a])
            total = term if total is None else total + term
        return total

    win[0] = jnp.where((column * time_ok) > 0.0, filter_with(xs, c1), 0.0).astype(BF)

    for copy, there, _ in shot_copies:
        @pl.when(there)
        def _(copy=copy):
            copy.start()

    lanes2 = iota((1, 2 * L), 1)

    def make_planes(offset, there):
        values = win[SLOT[offset]].astype(F32)
        if there is not None:
            values = jnp.where(there, values, 0.0)
        a = offset + SHOT_TAPS // 2
        planes[a] = pltpu.roll(values, GAP * a + 33, 1).astype(BF)
        p = a + SHOT_TAPS
        delay = dith[lax.rem(s + offset + shots, shots)]
        moved = pltpu.roll(values, GAP * p + 33 - delay, 1)
        early = (lanes2 >= GAP * p) & (lanes2 < GAP * p + 33)
        planes[p] = jnp.where(jnp.where(early, left_f, 1.0) > 0.0, moved, 0.0).astype(BF)

    same_half = (iota((L, L), 0) >= CH) == (iota((L, L), 1) >= CH)
    zero_block = jnp.zeros((L, L), BF)
    for layer in range(HID):
        weights = hw[layer]
        doubled = jnp.concatenate([weights, weights], axis=0)
        wh[layer, 3 * L :, 0:L] = zero_block
        wh[layer, 0:L, L:] = zero_block
        for k in range(3):
            pick = iota((L, 3 * CH), 1) == (k * CH + (iota((L, 3 * CH), 0) & (CH - 1)))
            block = jnp.where(same_half, dot_nt(pick.astype(BF), doubled), 0.0).astype(BF)
            wh[layer, k * L : (k + 1) * L, 0:L] = block
            wh[layer, (k + 1) * L : (k + 2) * L, L:] = block

    pick = iota((L, CH), 1) == (iota((L, CH), 0) & (CH - 1))
    spread = dot_nt(pick.astype(BF), jnp.broadcast_to(ow[...], (L, CH)))
    for r in range(4):
        for i in range(2):
            step = 8 * i + 2 * r
            here = (iota((L, L), 1) & 15) == step + jnp.where(iota((L, L), 0) >= CH, 1, 0)
            wo[(2 * r + i) * L : (2 * r + i + 1) * L, :] = jnp.where(here, spread, 0.0).astype(BF)

    def wide(bias):
        both = jnp.concatenate([bias, bias], axis=1)
        return jnp.concatenate([both, both], axis=1)

    first_bias = wide(fb[...])
    hidden_bias = [wide(hb[layer : layer + 1, :]) for layer in range(HID)]
    make_planes(0, None)

    def keep_second(a, near, far):
        c2[a, 0:L, :] = near
        c2[a, L:, :] = far

    circulants(shp[...], keep_second)
    for i, offset in ((2, -1), (3, 1), (0, -2), (1, 2)):
        copy, _, behind = shot_copies[i]

        @pl.when(behind)
        def _(copy=copy):
            copy.wait_recv()
        make_planes(offset, behind)

    for part in range(2):
        rows = slice(part * 32, part * 32 + 32)
        held = [planes[p, rows, :].astype(F32) for p in range(2 * SHOT_TAPS)]
        for g in range(GROUPS):
            place = (lanes2 - 16 * g) & 255
            merged = held[0]
            for p in range(1, 2 * SHOT_TAPS):
                merged = jnp.where(place >= GAP * p, held[p], merged)
            if g:
                merged = pltpu.roll(merged, 256 - 16 * g, 1)
            gs[g, rows, :] = merged.astype(BF)

    def finish(total, bias, factor):
        act = jnp.maximum(total + bias, 0.0)
        if factor is not None:
            act = act * factor
        return act.astype(BF)

    for g0, g1, factor in ((0, 2, left_f), (2, 6, None), (6, 10, None), (10, 12, right_f)):
        left = gs[g0:g1].reshape((g1 - g0) * N, 256)
        for quarter in range(4):
            act = finish(dot_nn(left, w0[:, quarter * 256 : (quarter + 1) * 256]), first_bias, factor)
            for g in range(g0, g1):
                for i in range(2):
                    at = (g - g0) * N
                    a0[8 * g + 2 * quarter + i] = act[at : at + N, i * L : (i + 1) * L]

    def chunks(lo, hi, size):
        cuts = [lo, 16 // size, 80 // size, hi]
        return [(cuts[0], cuts[1], left_f), (cuts[1], cuts[2], None), (cuts[2], cuts[3], right_f)]

    def layer(source, target, index, lo, hi, most):
        step = 1 << index
        for start, stop, factor in chunks(lo, hi, 2 * step):
            for j0 in range(start, stop, most):
                js = range(j0, min(j0 + most, stop))
                us = [2 * step * j + r for j in js for r in range(step)]
                left = jnp.concatenate(
                    [jnp.concatenate([source[u - step], source[u], source[u + step], source[u + 2 * step]], axis=1)
                     for u in us], axis=0)
                act = finish(dot_nn(left, wh[index]), hidden_bias[index], factor)
                target(us, step, act)

    def into(ref):
        def keep(us, step, act):
            for m, u in enumerate(us):
                ref[u] = act[m * N : (m + 1) * N, 0:L]
                ref[u + step] = act[m * N : (m + 1) * N, L:]
        return keep

    out_bias = ob[0]
    sixteen = lax.shift_right_logical(lane, 4)

    def last(us, step, act):
        for m, u in enumerate(us):
            r = m % step
            a3[u // 8 - 1, :, 2 * L * r : 2 * L * (r + 1)] = act[m * N : (m + 1) * N]

    layer(a0, into(a1), 0, 1, 47, 8)
    layer(a1, into(a2), 1, 1, 23, 4)
    layer(a2, last, 2, 1, 11, 2)
    scores = (dot_nn(a3[...].reshape(10 * N, 8 * L), wo[...]) + out_bias).astype(BF).astype(F32)
    pred = {j: scores[(j - 1) * N : j * N] for j in range(1, 11)}

    middle = pred[2]
    for j in range(3, 10):
        middle = jnp.where(sixteen == j - 2, pred[j], middle)
    middle = jnp.where(alive, middle, 0.0)
    out[0] = middle.astype(BF)
    edge = jnp.where(lane < 80, pred[10], pred[1])
    edge = jnp.where(alive_halo, edge, 0.0)
    rest = (win[0].astype(F32) - jnp.concatenate([middle, edge], axis=1)).astype(BF).astype(F32)
    ds[0:8, :] = jnp.zeros((8, 2 * L), F32)
    ds[72:80, :] = jnp.zeros((8, 2 * L), F32)
    ds[8:72, :] = rest
    out[1] = jnp.where(alive, filter_with(ds, c2), 0.0).astype(BF)

    for here, copy in (
        (has_right, to_right),
        (has_left, to_left),
        *[(there, copy) for copy, there, _ in shot_copies],
    ):
        @pl.when(here)
        def _(copy=copy):
            copy.wait_send()


def local(shots, tms, records, live, dither, designature, first_weights, first_bias, hidden_weights, hidden_bias,
          out_weights, out_bias, shaping):
    vmem = pl.BlockSpec(memory_space=pltpu.VMEM)
    hbm = pl.BlockSpec(memory_space=pltpu.HBM)
    shape = pltpu.VMEM((2, N, L), BF)
    inputs = (
        records.reshape(N, L),
        live,
        dither,
        designature,
        first_weights.T,
        first_bias.reshape(1, CH),
        hidden_weights,
        hidden_bias,
        out_weights.reshape(1, CH),
        out_bias,
        shaping,
    )
    spaces = [pltpu.SMEM if i in (2, 9) else pltpu.VMEM for i in range(len(inputs))]
    both = pl.pallas_call(
        functools.partial(kernel, shots, tms),
        out_shape=shape,
        in_specs=[hbm] * len(inputs),
        out_specs=vmem,
        scratch_shapes=[
            *[space(x.shape, x.dtype) for space, x in zip(spaces, inputs)],
            pltpu.VMEM((2, N, L), BF),
            pltpu.VMEM((5, N, 2 * L), BF),
            pltpu.VMEM((80, 2 * L), F32),
            pltpu.VMEM((FN, 2 * L, 2 * L), BF),
            pltpu.VMEM((FN, 2 * L, L), BF),
            pltpu.VMEM((256, 1024), BF),
            pltpu.VMEM((HID, 4 * L, 2 * L), BF),
            pltpu.VMEM((1024, L), BF),
            pltpu.VMEM((272, L), F32),
            pltpu.VMEM((2 * SHOT_TAPS, N, 2 * L), BF),
            pltpu.VMEM((GROUPS, N, 2 * L), BF),
            pltpu.VMEM((US, N, L), BF),
            pltpu.VMEM((US, N, L), BF),
            pltpu.VMEM((US, N, L), BF),
            pltpu.VMEM((10, N, 8 * L), BF),
            pltpu.VMEM((80, 2 * L), F32),
            pltpu.SemaphoreType.DMA((len(inputs),)),
            pltpu.SemaphoreType.DMA((2,)),
            pltpu.SemaphoreType.DMA((2,)),
            pltpu.SemaphoreType.DMA((4,)),
            pltpu.SemaphoreType.DMA((4,)),
        ],
        compiler_params=pltpu.CompilerParams(
            collective_id=0, has_side_effects=True, vmem_limit_bytes=61 * 1024 * 1024
        ),
    )(*inputs)
    return both[0:1], both[1:2]


def solution(mesh):
    shots, tms = mesh.shape["shot"], mesh.shape["tm"]
    in_specs = (P("shot", None, "tm"), P("shot", None), P(), P(), P(), P(), P(), P(), P(), P(), P())
    out_specs = (P("shot", None, "tm"), P("shot", None, "tm"))
    return jax.shard_map(
        functools.partial(local, shots, tms), mesh=mesh, in_specs=in_specs, out_specs=out_specs, check_vma=False
    )
```

```python
import functools

import jax
import jax.numpy as jnp
from jax import lax
from jax.experimental import pallas as pl
from jax.experimental.pallas import tpu as pltpu
from jax.sharding import PartitionSpec as P

HID = 3
FN = 9
FT = 33
SHOT_TAPS = 5
CH = 64
N = 64
L = 128
GAP = 24
GROUPS = 12
US = 8 * GROUPS
SLOT = {0: 0, -1: 1, 1: 2, -2: 3, 2: 4}
MESH = pl.DeviceIdType.MESH
BF = jnp.bfloat16
F32 = jnp.float32


def iota(shape, dim):
    return lax.broadcasted_iota(jnp.int32, shape, dim)


def dot_nn(a, b):
    return jnp.dot(a, b, preferred_element_type=F32)


def dot_nt(a, b):
    return lax.dot_general(a, b, (((1,), (1,)), ((), ())), preferred_element_type=F32)


def circulants(taps, store):
    pick = iota((FT, L), 0) == ((FT // 2 - iota((FT, L), 1)) & (L - 1))
    rows = dot_nn(taps, pick.astype(BF))
    near = jnp.abs(iota((L, L), 0) - iota((L, L), 1)) <= L // 2
    for a in range(FN):
        full = jnp.broadcast_to(rows[a : a + 1, :], (L, L))
        full = pltpu.roll(full, 0, 1, stride=1, stride_axis=0)
        store(a, jnp.where(near, full, 0.0).astype(BF), jnp.where(near, 0.0, full).astype(BF))


def kernel(
    shots,
    tms,
    rec_hbm,
    live_hbm,
    dith_hbm,
    des_hbm,
    fw_hbm,
    fb_hbm,
    hw_hbm,
    hb_hbm,
    ow_hbm,
    ob_hbm,
    shp_hbm,
    out,
    rec,
    live,
    dith,
    des,
    fw,
    fb,
    hw,
    hb,
    ow,
    ob,
    shp,
    halos,
    win,
    xs,
    c1,
    c2,
    w0,
    wh,
    wo,
    b0s,
    planes,
    gs,
    a0,
    a1,
    a2,
    a3,
    ds,
    in_sem,
    tm_send,
    tm_recv,
    shot_send,
    shot_recv,
    near_sem,
):
    s, z = lax.axis_index("shot"), lax.axis_index("tm")
    has_left, has_right = z > 0, z < tms - 1
    has_before, has_after = s > 0, s < shots - 1
    has_before2, has_after2 = s > 1, s < shots - 2

    barrier = pltpu.get_barrier_semaphore()
    expected = 0
    for here, device in (
        (has_left, (s, z - 1)),
        (has_right, (s, z + 1)),
        (has_before, (s - 1, z)),
        (has_after, (s + 1, z)),
    ):
        @pl.when(here)
        def _(device=device):
            pl.semaphore_signal(barrier, inc=1, device_id=device, device_id_type=MESH)
        expected = expected + here.astype(jnp.int32)

    fetches = [
        pltpu.make_async_copy(src, dst, in_sem.at[i])
        for i, (src, dst) in enumerate((
            (des_hbm, des), (rec_hbm, rec), (live_hbm, live), (fw_hbm, fw), (hw_hbm, hw), (dith_hbm, dith),
            (ow_hbm, ow), (shp_hbm, shp), (fb_hbm, fb), (hb_hbm, hb), (ob_hbm, ob)))
    ]
    for fetch in fetches:
        fetch.start()

    def remote(src, dst, send_sem, recv_sem, device):
        return pltpu.make_async_remote_copy(
            src_ref=src, dst_ref=dst, send_sem=send_sem, recv_sem=recv_sem,
            device_id=device, device_id_type=MESH,
        )

    to_right = remote(rec_hbm, halos.at[0], tm_send.at[0], tm_recv.at[0], (s, z + 1))
    to_left = remote(rec_hbm, halos.at[1], tm_send.at[1], tm_recv.at[1], (s, z - 1))

    def to_shot(index, offset):
        return remote(
            win.at[0], win.at[SLOT[-offset]], shot_send.at[index], shot_recv.at[index], (s + offset, z))

    shot_copies = [
        (to_shot(i, offset), there, behind)
        for i, (offset, there, behind) in enumerate((
            (2, has_after2, has_before2),
            (-2, has_before2, has_after2),
            (1, has_after, has_before),
            (-1, has_before, has_after)))
    ]

    def keep_first(a, near, far):
        c1[a, 0:L, 0:L] = near
        c1[a, 0:L, L:] = far
        c1[a, L:, 0:L] = far
        c1[a, L:, L:] = near

    pl.semaphore_wait(barrier, expected)

    @pl.when(has_right)
    def _():
        to_right.start()

    @pl.when(has_left)
    def _():
        to_left.start()

    @pl.when(has_before & has_after)
    def _():
        pl.semaphore_signal(near_sem.at[0], inc=1, device_id=(s - 1, z), device_id_type=MESH)
        pl.semaphore_signal(near_sem.at[1], inc=1, device_id=(s + 1, z), device_id_type=MESH)

    for fetch in fetches:
        fetch.wait()
    circulants(des[...], keep_first)

    lane = iota((1, L), 1)
    left_f, right_f = jnp.where(has_left, 1.0, 0.0), jnp.where(has_right, 1.0, 0.0)
    halo = jnp.where(lane < 80, right_f, left_f)
    time_ok = jnp.concatenate([jnp.ones((1, L), F32), halo], axis=1)
    diagonal = iota((N, N), 0) == iota((N, N), 1)
    spread_rows = jnp.where(diagonal, jnp.broadcast_to(live[...].astype(F32), (N, N)), 0.0)
    column = jnp.sum(spread_rows, axis=1, keepdims=True)
    alive = column > 0.0
    alive_halo = (column * halo) > 0.0

    xs[0:8, :] = jnp.zeros((8, 2 * L), F32)
    xs[72:80, :] = jnp.zeros((8, 2 * L), F32)
    xs[8:72, 0:L] = jnp.where(alive, rec[...].astype(F32), 0.0)

    upper = lane >= CH
    row, col = iota((256, 6 * SHOT_TAPS), 0), iota((256, 6 * SHOT_TAPS), 1)
    third = lax.shift_right_logical(col * 43, 7)
    place = row == GAP * third + (col - 3 * third)
    base = dot_nn(place.astype(BF), fw[...])
    b0s[0:16, :] = jnp.zeros((16, L), F32)
    b0s[16:, :] = jnp.concatenate([base, base], axis=1)
    for pair in range(8):
        even, odd = b0s[pl.ds(16 - 2 * pair, 256), :], b0s[pl.ds(15 - 2 * pair, 256), :]
        w0[:, pair * L : (pair + 1) * L] = jnp.where(upper, odd, even).astype(BF)

    @pl.when(has_left)
    def _():
        to_right.wait_recv()

    @pl.when(has_right)
    def _():
        to_left.wait_recv()

    sides = jnp.where(lane < 80, halos[1].astype(F32), halos[0].astype(F32))
    xs[8:72, L:] = jnp.where(alive_halo, sides, 0.0)

    def filter_with(source, matrices):
        total = None
        for a in range(FN):
            term = dot_nn(source[pl.ds(4 + a, N), :].astype(BF), matrices[a])
            total = term if total is None else total + term
        return total

    win[0] = jnp.where((column * time_ok) > 0.0, filter_with(xs, c1), 0.0).astype(BF)

    for i, (copy, there, _) in enumerate(shot_copies):
        @pl.when(there)
        def _(i=i, copy=copy):
            if i < 2:
                pl.semaphore_wait(near_sem.at[i], 1)
            copy.start()

    lanes2 = iota((1, 2 * L), 1)

    def make_planes(offset, there):
        values = win[SLOT[offset]].astype(F32)
        if there is not None:
            values = jnp.where(there, values, 0.0)
        a = offset + SHOT_TAPS // 2
        planes[a] = pltpu.roll(values, GAP * a + 33, 1).astype(BF)
        p = a + SHOT_TAPS
        delay = dith[lax.rem(s + offset + shots, shots)]
        moved = pltpu.roll(values, GAP * p + 33 - delay, 1)
        early = (lanes2 >= GAP * p) & (lanes2 < GAP * p + 33)
        planes[p] = jnp.where(jnp.where(early, left_f, 1.0) > 0.0, moved, 0.0).astype(BF)

    same_half = (iota((L, L), 0) >= CH) == (iota((L, L), 1) >= CH)
    zero_block = jnp.zeros((L, L), BF)
    for layer in range(HID):
        weights = hw[layer]
        doubled = jnp.concatenate([weights, weights], axis=0)
        wh[layer, 3 * L :, 0:L] = zero_block
        wh[layer, 0:L, L:] = zero_block
        for k in range(3):
            pick = iota((L, 3 * CH), 1) == (k * CH + (iota((L, 3 * CH), 0) & (CH - 1)))
            block = jnp.where(same_half, dot_nt(pick.astype(BF), doubled), 0.0).astype(BF)
            wh[layer, k * L : (k + 1) * L, 0:L] = block
            wh[layer, (k + 1) * L : (k + 2) * L, L:] = block

    pick = iota((L, CH), 1) == (iota((L, CH), 0) & (CH - 1))
    spread = dot_nt(pick.astype(BF), jnp.broadcast_to(ow[...], (L, CH)))
    for r in range(4):
        for i in range(2):
            step = 8 * i + 2 * r
            here = (iota((L, L), 1) & 15) == step + jnp.where(iota((L, L), 0) >= CH, 1, 0)
            wo[(2 * r + i) * L : (2 * r + i + 1) * L, :] = jnp.where(here, spread, 0.0).astype(BF)

    def wide(bias):
        both = jnp.concatenate([bias, bias], axis=1)
        return jnp.concatenate([both, both], axis=1)

    first_bias = wide(fb[...])
    hidden_bias = [wide(hb[layer : layer + 1, :]) for layer in range(HID)]
    make_planes(0, None)

    def keep_second(a, near, far):
        c2[a, 0:L, :] = near
        c2[a, L:, :] = far

    circulants(shp[...], keep_second)
    for i, offset in ((2, -1), (3, 1), (0, -2), (1, 2)):
        copy, _, behind = shot_copies[i]

        @pl.when(behind)
        def _(copy=copy):
            copy.wait_recv()
        make_planes(offset, behind)

    for part in range(2):
        rows = slice(part * 32, part * 32 + 32)
        held = [planes[p, rows, :].astype(F32) for p in range(2 * SHOT_TAPS)]
        for g in range(GROUPS):
            place = (lanes2 - 16 * g) & 255
            merged = held[0]
            for p in range(1, 2 * SHOT_TAPS):
                merged = jnp.where(place >= GAP * p, held[p], merged)
            if g:
                merged = pltpu.roll(merged, 256 - 16 * g, 1)
            gs[g, rows, :] = merged.astype(BF)

    def finish(total, bias, factor):
        act = jnp.maximum(total + bias, 0.0)
        if factor is not None:
            act = act * factor
        return act.astype(BF)

    for g0, g1, factor in ((0, 2, left_f), (2, 6, None), (6, 10, None), (10, 12, right_f)):
        left = gs[g0:g1].reshape((g1 - g0) * N, 256)
        for quarter in range(4):
            act = finish(dot_nn(left, w0[:, quarter * 256 : (quarter + 1) * 256]), first_bias, factor)
            for g in range(g0, g1):
                for i in range(2):
                    at = (g - g0) * N
                    a0[8 * g + 2 * quarter + i] = act[at : at + N, i * L : (i + 1) * L]

    def chunks(lo, hi, size):
        cuts = [lo, 16 // size, 80 // size, hi]
        return [(cuts[0], cuts[1], left_f), (cuts[1], cuts[2], None), (cuts[2], cuts[3], right_f)]

    def layer(source, target, index, lo, hi, most):
        step = 1 << index
        for start, stop, factor in chunks(lo, hi, 2 * step):
            for j0 in range(start, stop, most):
                js = range(j0, min(j0 + most, stop))
                us = [2 * step * j + r for j in js for r in range(step)]
                left = jnp.concatenate(
                    [jnp.concatenate([source[u - step], source[u], source[u + step], source[u + 2 * step]], axis=1)
                     for u in us], axis=0)
                act = finish(dot_nn(left, wh[index]), hidden_bias[index], factor)
                target(us, step, act)

    def into(ref):
        def keep(us, step, act):
            for m, u in enumerate(us):
                ref[u] = act[m * N : (m + 1) * N, 0:L]
                ref[u + step] = act[m * N : (m + 1) * N, L:]
        return keep

    out_bias = ob[...]
    sixteen = lax.shift_right_logical(lane, 4)

    def last(us, step, act):
        for m, u in enumerate(us):
            r = m % step
            a3[u // 8 - 1, :, 2 * L * r : 2 * L * (r + 1)] = act[m * N : (m + 1) * N]

    layer(a0, into(a1), 0, 1, 47, 8)
    layer(a1, into(a2), 1, 1, 23, 4)
    layer(a2, last, 2, 1, 11, 2)
    scores = (dot_nn(a3[...].reshape(10 * N, 8 * L), wo[...]) + out_bias).astype(BF).astype(F32)
    pred = {j: scores[(j - 1) * N : j * N] for j in range(1, 11)}

    middle = pred[2]
    for j in range(3, 10):
        middle = jnp.where(sixteen == j - 2, pred[j], middle)
    middle = jnp.where(alive, middle, 0.0)
    out[0] = middle.astype(BF)
    edge = jnp.where(lane < 80, pred[10], pred[1])
    edge = jnp.where(alive_halo, edge, 0.0)
    rest = (win[0].astype(F32) - jnp.concatenate([middle, edge], axis=1)).astype(BF).astype(F32)
    ds[0:8, :] = jnp.zeros((8, 2 * L), F32)
    ds[72:80, :] = jnp.zeros((8, 2 * L), F32)
    ds[8:72, :] = rest
    out[1] = jnp.where(alive, filter_with(ds, c2), 0.0).astype(BF)

    for here, copy in (
        (has_right, to_right),
        (has_left, to_left),
        *[(there, copy) for copy, there, _ in shot_copies],
    ):
        @pl.when(here)
        def _(copy=copy):
            copy.wait_send()


def local(shots, tms, records, live, dither, designature, first_weights, first_bias, hidden_weights, hidden_bias,
          out_weights, out_bias, shaping):
    vmem = pl.BlockSpec(memory_space=pltpu.VMEM)
    hbm = pl.BlockSpec(memory_space=pltpu.HBM)
    shape = pltpu.VMEM((2, N, L), BF)
    inputs = (
        records.reshape(N, L),
        live,
        dither,
        designature,
        first_weights.T,
        first_bias.reshape(1, CH),
        hidden_weights,
        hidden_bias,
        out_weights.reshape(1, CH),
        out_bias.reshape(1, 1),
        shaping,
    )
    spaces = [pltpu.SMEM if i == 2 else pltpu.VMEM for i in range(len(inputs))]
    both = pl.pallas_call(
        functools.partial(kernel, shots, tms),
        out_shape=shape,
        in_specs=[hbm] * len(inputs),
        out_specs=vmem,
        scratch_shapes=[
            *[space(x.shape, x.dtype) for space, x in zip(spaces, inputs)],
            pltpu.VMEM((2, N, L), BF),
            pltpu.VMEM((5, N, 2 * L), BF),
            pltpu.VMEM((80, 2 * L), F32),
            pltpu.VMEM((FN, 2 * L, 2 * L), BF),
            pltpu.VMEM((FN, 2 * L, L), BF),
            pltpu.VMEM((256, 1024), BF),
            pltpu.VMEM((HID, 4 * L, 2 * L), BF),
            pltpu.VMEM((1024, L), BF),
            pltpu.VMEM((272, L), F32),
            pltpu.VMEM((2 * SHOT_TAPS, N, 2 * L), BF),
            pltpu.VMEM((GROUPS, N, 2 * L), BF),
            pltpu.VMEM((US, N, L), BF),
            pltpu.VMEM((US, N, L), BF),
            pltpu.VMEM((US, N, L), BF),
            pltpu.VMEM((10, N, 8 * L), BF),
            pltpu.VMEM((80, 2 * L), F32),
            pltpu.SemaphoreType.DMA((len(inputs),)),
            pltpu.SemaphoreType.DMA((2,)),
            pltpu.SemaphoreType.DMA((2,)),
            pltpu.SemaphoreType.DMA((4,)),
            pltpu.SemaphoreType.DMA((4,)),
            pltpu.SemaphoreType.REGULAR((2,)),
        ],
        compiler_params=pltpu.CompilerParams(
            collective_id=0, has_side_effects=True, vmem_limit_bytes=61 * 1024 * 1024
        ),
    )(*inputs)
    return both[0:1], both[1:2]


def solution(mesh):
    shots, tms = mesh.shape["shot"], mesh.shape["tm"]
    in_specs = (P("shot", None, "tm"), P("shot", None), P(), P(), P(), P(), P(), P(), P(), P(), P())
    out_specs = (P("shot", None, "tm"), P("shot", None, "tm"))
    return jax.shard_map(
        functools.partial(local, shots, tms), mesh=mesh, in_specs=in_specs, out_specs=out_specs, check_vma=False
    )
```

```python
import functools

import jax
import jax.numpy as jnp
from jax import lax
from jax.experimental import pallas as pl
from jax.experimental.pallas import tpu as pltpu
from jax.sharding import PartitionSpec as P

HID = 3
FN = 9
FT = 33
SHOT_TAPS = 5
CH = 64
N = 64
L = 128
GAP = 24
GROUPS = 12
US = 8 * GROUPS
SLOT = {0: 0, -1: 1, 1: 2, -2: 3, 2: 4}
MESH = pl.DeviceIdType.MESH
BF = jnp.bfloat16
F32 = jnp.float32


def iota(shape, dim):
    return lax.broadcasted_iota(jnp.int32, shape, dim)


def dot_nn(a, b):
    return jnp.dot(a, b, preferred_element_type=F32)


def dot_nt(a, b):
    return lax.dot_general(a, b, (((1,), (1,)), ((), ())), preferred_element_type=F32)


def circulants(taps, store):
    pick = iota((FT, L), 0) == ((FT // 2 - iota((FT, L), 1)) & (L - 1))
    rows = dot_nn(taps, pick.astype(BF))
    near = jnp.abs(iota((L, L), 0) - iota((L, L), 1)) <= L // 2
    for a in range(FN):
        full = jnp.broadcast_to(rows[a : a + 1, :], (L, L))
        full = pltpu.roll(full, 0, 1, stride=1, stride_axis=0)
        store(a, jnp.where(near, full, 0.0).astype(BF), jnp.where(near, 0.0, full).astype(BF))


def kernel(
    shots,
    tms,
    rec_hbm,
    live_hbm,
    dith_hbm,
    des_hbm,
    fw_hbm,
    fb_hbm,
    hw_hbm,
    hb_hbm,
    ow_hbm,
    ob_hbm,
    shp_hbm,
    out,
    rec,
    live,
    dith,
    des,
    fw,
    fb,
    hw,
    hb,
    ow,
    ob,
    shp,
    halos,
    inner,
    outer,
    win,
    xs,
    c1,
    c2,
    w0,
    wh,
    wo,
    b0s,
    planes,
    gs,
    a0,
    a1,
    a2,
    a3,
    ds,
    in_sem,
    tm_send,
    tm_recv,
    shot_send,
    shot_recv,
    near_sem,
):
    s, z = lax.axis_index("shot"), lax.axis_index("tm")
    has_left, has_right = z > 0, z < tms - 1
    has_before, has_after = s > 0, s < shots - 1
    has_before2, has_after2 = s > 1, s < shots - 2

    barrier = pltpu.get_barrier_semaphore()
    expected = 0
    for here, device in (
        (has_left, (s, z - 1)),
        (has_right, (s, z + 1)),
        (has_before, (s - 1, z)),
        (has_after, (s + 1, z)),
    ):
        @pl.when(here)
        def _(device=device):
            pl.semaphore_signal(barrier, inc=1, device_id=device, device_id_type=MESH)
        expected = expected + here.astype(jnp.int32)

    fetches = [
        pltpu.make_async_copy(src, dst, in_sem.at[i])
        for i, (src, dst) in enumerate((
            (des_hbm, des), (rec_hbm, rec), (live_hbm, live), (fw_hbm, fw), (hw_hbm, hw), (dith_hbm, dith),
            (ow_hbm, ow), (shp_hbm, shp), (fb_hbm, fb), (hb_hbm, hb), (ob_hbm, ob)))
    ]
    for fetch in fetches:
        fetch.start()

    def remote(src, dst, send_sem, recv_sem, device):
        return pltpu.make_async_remote_copy(
            src_ref=src, dst_ref=dst, send_sem=send_sem, recv_sem=recv_sem,
            device_id=device, device_id_type=MESH,
        )

    to_right = remote(rec_hbm, halos.at[0], tm_send.at[0], tm_recv.at[0], (s, z + 1))
    to_left = remote(rec_hbm, halos.at[1], tm_send.at[1], tm_recv.at[1], (s, z - 1))

    def to_shot(index, offset, part):
        return remote(
            part.at[0], part.at[SLOT[-offset]], shot_send.at[index], shot_recv.at[index], (s + offset, z))

    reach = ((2, has_after2, has_before2), (-2, has_before2, has_after2), (1, has_after, has_before),
             (-1, has_before, has_after))
    inner_copies = [(to_shot(i, o, inner), there, behind) for i, (o, there, behind) in enumerate(reach)]
    outer_copies = [(to_shot(4 + i, o, outer), there, behind) for i, (o, there, behind) in enumerate(reach)]

    def keep_first(a, near, far):
        c1[a, 0:L, 0:L] = near
        c1[a, 0:L, L:] = far
        c1[a, L:, 0:L] = far
        c1[a, L:, L:] = near

    pl.semaphore_wait(barrier, expected)

    @pl.when(has_right)
    def _():
        to_right.start()

    @pl.when(has_left)
    def _():
        to_left.start()

    @pl.when(has_before & has_after)
    def _():
        pl.semaphore_signal(near_sem.at[0], inc=1, device_id=(s - 1, z), device_id_type=MESH)
        pl.semaphore_signal(near_sem.at[1], inc=1, device_id=(s + 1, z), device_id_type=MESH)

    for fetch in fetches:
        fetch.wait()
    circulants(des[...], keep_first)

    lane = iota((1, L), 1)
    left_f, right_f = jnp.where(has_left, 1.0, 0.0), jnp.where(has_right, 1.0, 0.0)
    halo = jnp.where(lane < 80, right_f, left_f)
    time_ok = jnp.concatenate([jnp.ones((1, L), F32), halo], axis=1)
    diagonal = iota((N, N), 0) == iota((N, N), 1)
    spread_rows = jnp.where(diagonal, jnp.broadcast_to(live[...].astype(F32), (N, N)), 0.0)
    column = jnp.sum(spread_rows, axis=1, keepdims=True)
    alive = column > 0.0
    alive_halo = (column * halo) > 0.0

    xs[0:8, :] = jnp.zeros((8, 2 * L), F32)
    xs[72:80, :] = jnp.zeros((8, 2 * L), F32)
    xs[8:72, 0:L] = jnp.where(alive, rec[...].astype(F32), 0.0)

    upper = lane >= CH
    row, col = iota((256, 6 * SHOT_TAPS), 0), iota((256, 6 * SHOT_TAPS), 1)
    third = lax.shift_right_logical(col * 43, 7)
    place = row == GAP * third + (col - 3 * third)
    base = dot_nn(place.astype(BF), fw[...])
    b0s[0:16, :] = jnp.zeros((16, L), F32)
    b0s[16:, :] = jnp.concatenate([base, base], axis=1)
    for pair in range(8):
        even, odd = b0s[pl.ds(16 - 2 * pair, 256), :], b0s[pl.ds(15 - 2 * pair, 256), :]
        w0[:, pair * L : (pair + 1) * L] = jnp.where(upper, odd, even).astype(BF)

    def filter_with(source, half, matrices, total=None):
        part = slice(half * L, half * L + L)
        for a in range(FN):
            term = dot_nn(source[pl.ds(4 + a, N), part].astype(BF), matrices[a, part, :])
            total = term if total is None else total + term
        return total

    started = filter_with(xs, 0, c1)
    inner[0] = jnp.where(alive, started[:, 0:L], 0.0).astype(BF)
    for i, (copy, there, _) in enumerate(inner_copies):
        @pl.when(there)
        def _(i=i, copy=copy):
            if i < 2:
                pl.semaphore_wait(near_sem.at[i], 1)
            copy.start()

    @pl.when(has_left)
    def _():
        to_right.wait_recv()

    @pl.when(has_right)
    def _():
        to_left.wait_recv()

    sides = jnp.where(lane < 80, halos[1].astype(F32), halos[0].astype(F32))
    xs[8:72, L:] = jnp.where(alive_halo, sides, 0.0)
    own = jnp.where((column * time_ok) > 0.0, filter_with(xs, 1, c1, started), 0.0)
    spare = (lane >= 64) & (lane < 96)
    outer[0] = jnp.where(spare, pltpu.roll(own[:, 0:L], L - 48, 1), own[:, L:]).astype(BF)
    for copy, there, _ in outer_copies:
        @pl.when(there)
        def _(copy=copy):
            copy.start()

    win[...] = own.astype(BF)

    lanes2 = iota((1, 2 * L), 1)

    def make_planes(offset, there):
        if offset == 0:
            values = win[...].astype(F32)
        else:
            slot = SLOT[offset]
            rim = outer[slot].astype(F32)
            middle = (lane >= 16) & (lane < 112)
            centre = jnp.where(middle, inner[slot].astype(F32), pltpu.roll(rim, 48, 1))
            values = jnp.where(there, jnp.concatenate([centre, rim], axis=1), 0.0)
        a = offset + SHOT_TAPS // 2
        planes[a] = pltpu.roll(values, GAP * a + 33, 1).astype(BF)
        p = a + SHOT_TAPS
        delay = dith[lax.rem(s + offset + shots, shots)]
        moved = pltpu.roll(values, GAP * p + 33 - delay, 1)
        early = (lanes2 >= GAP * p) & (lanes2 < GAP * p + 33)
        planes[p] = jnp.where(jnp.where(early, left_f, 1.0) > 0.0, moved, 0.0).astype(BF)

    same_half = (iota((L, L), 0) >= CH) == (iota((L, L), 1) >= CH)
    zero_block = jnp.zeros((L, L), BF)
    for layer in range(HID):
        weights = hw[layer]
        doubled = jnp.concatenate([weights, weights], axis=0)
        wh[layer, 3 * L :, 0:L] = zero_block
        wh[layer, 0:L, L:] = zero_block
        for k in range(3):
            pick = iota((L, 3 * CH), 1) == (k * CH + (iota((L, 3 * CH), 0) & (CH - 1)))
            block = jnp.where(same_half, dot_nt(pick.astype(BF), doubled), 0.0).astype(BF)
            wh[layer, k * L : (k + 1) * L, 0:L] = block
            wh[layer, (k + 1) * L : (k + 2) * L, L:] = block

    pick = iota((L, CH), 1) == (iota((L, CH), 0) & (CH - 1))
    spread = dot_nt(pick.astype(BF), jnp.broadcast_to(ow[...], (L, CH)))
    for r in range(4):
        for i in range(2):
            step = 8 * i + 2 * r
            here = (iota((L, L), 1) & 15) == step + jnp.where(iota((L, L), 0) >= CH, 1, 0)
            wo[(2 * r + i) * L : (2 * r + i + 1) * L, :] = jnp.where(here, spread, 0.0).astype(BF)

    def wide(bias):
        both = jnp.concatenate([bias, bias], axis=1)
        return jnp.concatenate([both, both], axis=1)

    first_bias = wide(fb[...])
    hidden_bias = [wide(hb[layer : layer + 1, :]) for layer in range(HID)]
    make_planes(0, None)

    def keep_second(a, near, far):
        c2[a, 0:L, :] = near
        c2[a, L:, :] = far

    circulants(shp[...], keep_second)
    def merge(numbers, begin, last):
        for part in range(2):
            rows = slice(part * 32, part * 32 + 32)
            held = {p: planes[p, rows, :] for p in numbers}
            for g in range(GROUPS):
                place = ((lanes2 - 16 * g) & 255).astype(F32).astype(BF)
                merged = held[numbers[0]] if begin else gs[g, rows, :]
                for p in numbers[1:] if begin else numbers:
                    inside = (place >= GAP * p) & (place < GAP * p + GAP)
                    merged = jnp.where(inside, held[p], merged)
                if last and g:
                    merged = pltpu.roll(merged.astype(F32), 256 - 16 * g, 1).astype(BF)
                gs[g, rows, :] = merged

    def arrived(i, offset):
        inside, _, behind = inner_copies[i]
        beyond = outer_copies[i][0]

        @pl.when(behind)
        def _():
            inside.wait_recv()
            beyond.wait_recv()
        make_planes(offset, behind)

    arrived(2, -1)
    arrived(3, 1)
    merge((1, 2, 3, 6, 7, 8), True, False)
    arrived(0, -2)
    arrived(1, 2)
    merge((0, 4, 5, 9), False, True)

    def finish(total, bias, factor):
        act = jnp.maximum(total + bias, 0.0)
        if factor is not None:
            act = act * factor
        return act.astype(BF)

    for g0, g1, factor in ((0, 2, left_f), (2, 6, None), (6, 10, None), (10, 12, right_f)):
        left = gs[g0:g1].reshape((g1 - g0) * N, 256)
        for quarter in range(4):
            act = finish(dot_nn(left, w0[:, quarter * 256 : (quarter + 1) * 256]), first_bias, factor)
            for g in range(g0, g1):
                for i in range(2):
                    at = (g - g0) * N
                    a0[8 * g + 2 * quarter + i] = act[at : at + N, i * L : (i + 1) * L]

    def chunks(lo, hi, size):
        cuts = [lo, 16 // size, 80 // size, hi]
        return [(cuts[0], cuts[1], left_f), (cuts[1], cuts[2], None), (cuts[2], cuts[3], right_f)]

    def layer(source, target, index, lo, hi, most):
        step = 1 << index
        for start, stop, factor in chunks(lo, hi, 2 * step):
            for j0 in range(start, stop, most):
                js = range(j0, min(j0 + most, stop))
                us = [2 * step * j + r for j in js for r in range(step)]
                left = jnp.concatenate(
                    [jnp.concatenate([source[u - step], source[u], source[u + step], source[u + 2 * step]], axis=1)
                     for u in us], axis=0)
                act = finish(dot_nn(left, wh[index]), hidden_bias[index], factor)
                target(us, step, act)

    def into(ref):
        def keep(us, step, act):
            for m, u in enumerate(us):
                ref[u] = act[m * N : (m + 1) * N, 0:L]
                ref[u + step] = act[m * N : (m + 1) * N, L:]
        return keep

    out_bias = ob[...]
    sixteen = lax.shift_right_logical(lane, 4)

    def last(us, step, act):
        for m, u in enumerate(us):
            r = m % step
            a3[u // 8 - 1, :, 2 * L * r : 2 * L * (r + 1)] = act[m * N : (m + 1) * N]

    layer(a0, into(a1), 0, 1, 47, 8)
    layer(a1, into(a2), 1, 1, 23, 4)
    layer(a2, last, 2, 1, 11, 2)
    scores = (dot_nn(a3[...].reshape(10 * N, 8 * L), wo[...]) + out_bias).astype(BF).astype(F32)
    pred = {j: scores[(j - 1) * N : j * N] for j in range(1, 11)}

    middle = pred[2]
    for j in range(3, 10):
        middle = jnp.where(sixteen == j - 2, pred[j], middle)
    middle = jnp.where(alive, middle, 0.0)
    out[0] = middle.astype(BF)
    edge = jnp.where(lane < 80, pred[10], pred[1])
    edge = jnp.where(alive_halo, edge, 0.0)
    rest = (win[...].astype(F32) - jnp.concatenate([middle, edge], axis=1)).astype(BF).astype(F32)
    ds[0:8, :] = jnp.zeros((8, 2 * L), F32)
    ds[72:80, :] = jnp.zeros((8, 2 * L), F32)
    ds[8:72, :] = rest
    out[1] = jnp.where(alive, filter_with(ds, 1, c2, filter_with(ds, 0, c2)), 0.0).astype(BF)

    for here, copy in (
        (has_right, to_right),
        (has_left, to_left),
        *[(there, copy) for copy, there, _ in inner_copies + outer_copies],
    ):
        @pl.when(here)
        def _(copy=copy):
            copy.wait_send()


def local(shots, tms, records, live, dither, designature, first_weights, first_bias, hidden_weights, hidden_bias,
          out_weights, out_bias, shaping):
    vmem = pl.BlockSpec(memory_space=pltpu.VMEM)
    hbm = pl.BlockSpec(memory_space=pltpu.HBM)
    shape = pltpu.VMEM((2, N, L), BF)
    inputs = (
        records.reshape(N, L),
        live,
        dither,
        designature,
        first_weights.T,
        first_bias.reshape(1, CH),
        hidden_weights,
        hidden_bias,
        out_weights.reshape(1, CH),
        out_bias.reshape(1, 1),
        shaping,
    )
    spaces = [pltpu.SMEM if i == 2 else pltpu.VMEM for i in range(len(inputs))]
    both = pl.pallas_call(
        functools.partial(kernel, shots, tms),
        out_shape=shape,
        in_specs=[hbm] * len(inputs),
        out_specs=vmem,
        scratch_shapes=[
            *[space(x.shape, x.dtype) for space, x in zip(spaces, inputs)],
            pltpu.VMEM((2, N, L), BF),
            pltpu.VMEM((5, N, L), BF),
            pltpu.VMEM((5, N, L), BF),
            pltpu.VMEM((N, 2 * L), BF),
            pltpu.VMEM((80, 2 * L), F32),
            pltpu.VMEM((FN, 2 * L, 2 * L), BF),
            pltpu.VMEM((FN, 2 * L, L), BF),
            pltpu.VMEM((256, 1024), BF),
            pltpu.VMEM((HID, 4 * L, 2 * L), BF),
            pltpu.VMEM((1024, L), BF),
            pltpu.VMEM((272, L), F32),
            pltpu.VMEM((2 * SHOT_TAPS, N, 2 * L), BF),
            pltpu.VMEM((GROUPS, N, 2 * L), BF),
            pltpu.VMEM((US, N, L), BF),
            pltpu.VMEM((US, N, L), BF),
            pltpu.VMEM((US, N, L), BF),
            pltpu.VMEM((10, N, 8 * L), BF),
            pltpu.VMEM((80, 2 * L), F32),
            pltpu.SemaphoreType.DMA((len(inputs),)),
            pltpu.SemaphoreType.DMA((2,)),
            pltpu.SemaphoreType.DMA((2,)),
            pltpu.SemaphoreType.DMA((8,)),
            pltpu.SemaphoreType.DMA((8,)),
            pltpu.SemaphoreType.REGULAR((2,)),
        ],
        compiler_params=pltpu.CompilerParams(
            collective_id=0, has_side_effects=True, vmem_limit_bytes=61 * 1024 * 1024
        ),
    )(*inputs)
    return both[0:1], both[1:2]


def solution(mesh):
    shots, tms = mesh.shape["shot"], mesh.shape["tm"]
    in_specs = (P("shot", None, "tm"), P("shot", None), P(), P(), P(), P(), P(), P(), P(), P(), P())
    out_specs = (P("shot", None, "tm"), P("shot", None, "tm"))
    return jax.shard_map(
        functools.partial(local, shots, tms), mesh=mesh, in_specs=in_specs, out_specs=out_specs, check_vma=False
    )
```

```python
import functools

import jax
import jax.numpy as jnp
from jax import lax
from jax.experimental import pallas as pl
from jax.experimental.pallas import tpu as pltpu
from jax.sharding import PartitionSpec as P

HID = 3
FN = 9
FT = 33
SHOT_TAPS = 5
CH = 64
N = 64
L = 128
GAP = 24
GROUPS = 12
US = 8 * GROUPS
SLOT = {0: 0, -1: 1, 1: 2, -2: 3, 2: 4}
MESH = pl.DeviceIdType.MESH
BF = jnp.bfloat16
F32 = jnp.float32


def iota(shape, dim):
    return lax.broadcasted_iota(jnp.int32, shape, dim)


def dot_nn(a, b):
    return jnp.dot(a, b, preferred_element_type=F32)


def dot_nt(a, b):
    return lax.dot_general(a, b, (((1,), (1,)), ((), ())), preferred_element_type=F32)


def circulants(taps, store):
    pick = iota((FT, L), 0) == ((FT // 2 - iota((FT, L), 1)) & (L - 1))
    rows = dot_nn(taps, pick.astype(BF))
    near = jnp.abs(iota((L, L), 0) - iota((L, L), 1)) <= L // 2
    for a in range(FN):
        full = jnp.broadcast_to(rows[a : a + 1, :], (L, L))
        full = pltpu.roll(full, 0, 1, stride=1, stride_axis=0)
        store(a, jnp.where(near, full, 0.0).astype(BF), jnp.where(near, 0.0, full).astype(BF))


def kernel(
    shots,
    tms,
    rec_hbm,
    live_hbm,
    dith_hbm,
    des_hbm,
    fw_hbm,
    fb_hbm,
    hw_hbm,
    hb_hbm,
    ow_hbm,
    ob_hbm,
    shp_hbm,
    out,
    rec,
    live,
    dith,
    des,
    fw,
    fb,
    hw,
    hb,
    ow,
    ob,
    shp,
    halos,
    inner,
    outer,
    win,
    xs,
    c1,
    c2,
    w0,
    wh,
    wo,
    b0s,
    planes,
    gs,
    a0,
    a1,
    a2,
    a3,
    ds,
    in_sem,
    tm_send,
    tm_recv,
    shot_send,
    shot_recv,
    near_sem,
):
    s, z = lax.axis_index("shot"), lax.axis_index("tm")
    has_left, has_right = z > 0, z < tms - 1
    has_before, has_after = s > 0, s < shots - 1
    has_before2, has_after2 = s > 1, s < shots - 2

    barrier = pltpu.get_barrier_semaphore()
    expected = 0
    for here, device in (
        (has_left, (s, z - 1)),
        (has_right, (s, z + 1)),
        (has_before, (s - 1, z)),
        (has_after, (s + 1, z)),
    ):
        @pl.when(here)
        def _(device=device):
            pl.semaphore_signal(barrier, inc=1, device_id=device, device_id_type=MESH)
        expected = expected + here.astype(jnp.int32)

    fetches = [
        pltpu.make_async_copy(src, dst, in_sem.at[i])
        for i, (src, dst) in enumerate((
            (des_hbm, des), (rec_hbm, rec), (live_hbm, live), (fw_hbm, fw), (hw_hbm, hw), (dith_hbm, dith),
            (ow_hbm, ow), (shp_hbm, shp), (fb_hbm, fb), (hb_hbm, hb), (ob_hbm, ob)))
    ]
    for fetch in fetches:
        fetch.start()

    def remote(src, dst, send_sem, recv_sem, device):
        return pltpu.make_async_remote_copy(
            src_ref=src, dst_ref=dst, send_sem=send_sem, recv_sem=recv_sem,
            device_id=device, device_id_type=MESH,
        )

    to_right = remote(rec_hbm, halos.at[0], tm_send.at[0], tm_recv.at[0], (s, z + 1))
    to_left = remote(rec_hbm, halos.at[1], tm_send.at[1], tm_recv.at[1], (s, z - 1))

    def to_shot(index, offset, part):
        return remote(
            part.at[0], part.at[SLOT[-offset]], shot_send.at[index], shot_recv.at[index], (s + offset, z))

    reach = ((2, has_after2, has_before2), (-2, has_before2, has_after2), (1, has_after, has_before),
             (-1, has_before, has_after))
    inner_copies = [(to_shot(i, o, inner), there, behind) for i, (o, there, behind) in enumerate(reach)]
    outer_copies = [(to_shot(4 + i, o, outer), there, behind) for i, (o, there, behind) in enumerate(reach)]

    def keep_first(a, near, far):
        c1[a, 0:L, 0:L] = near
        c1[a, 0:L, L:] = far
        c1[a, L:, 0:L] = far
        c1[a, L:, L:] = near

    pl.semaphore_wait(barrier, expected)

    @pl.when(has_left)
    def _():
        to_left.start()

    @pl.when(has_right)
    def _():
        to_right.start()

    @pl.when(has_before & has_after)
    def _():
        pl.semaphore_signal(near_sem.at[0], inc=1, device_id=(s - 1, z), device_id_type=MESH)
        pl.semaphore_signal(near_sem.at[1], inc=1, device_id=(s + 1, z), device_id_type=MESH)

    for fetch in fetches:
        fetch.wait()
    circulants(des[...], keep_first)

    lane = iota((1, L), 1)
    left_f, right_f = jnp.where(has_left, 1.0, 0.0), jnp.where(has_right, 1.0, 0.0)
    halo = jnp.where(lane < 80, right_f, left_f)
    time_ok = jnp.concatenate([jnp.ones((1, L), F32), halo], axis=1)
    diagonal = iota((N, N), 0) == iota((N, N), 1)
    spread_rows = jnp.where(diagonal, jnp.broadcast_to(live[...].astype(F32), (N, N)), 0.0)
    column = jnp.sum(spread_rows, axis=1, keepdims=True)
    alive = column > 0.0
    alive_halo = (column * halo) > 0.0

    xs[0:8, :] = jnp.zeros((8, 2 * L), F32)
    xs[72:80, :] = jnp.zeros((8, 2 * L), F32)
    xs[8:72, 0:L] = jnp.where(alive, rec[...].astype(F32), 0.0)

    upper = lane >= CH
    row, col = iota((256, 6 * SHOT_TAPS), 0), iota((256, 6 * SHOT_TAPS), 1)
    third = lax.shift_right_logical(col * 43, 7)
    place = row == GAP * third + (col - 3 * third)
    base = dot_nn(place.astype(BF), fw[...])
    b0s[0:16, :] = jnp.zeros((16, L), F32)
    b0s[16:, :] = jnp.concatenate([base, base], axis=1)
    for pair in range(8):
        even, odd = b0s[pl.ds(16 - 2 * pair, 256), :], b0s[pl.ds(15 - 2 * pair, 256), :]
        w0[:, pair * L : (pair + 1) * L] = jnp.where(upper, odd, even).astype(BF)

    def filter_with(source, half, matrices, total=None):
        part = slice(0, 2 * L) if half is None else slice(half * L, half * L + L)
        for a in range(FN):
            term = dot_nn(source[pl.ds(4 + a, N), part].astype(BF), matrices[a, part, :])
            total = term if total is None else total + term
        return total

    started = filter_with(xs, 0, c1)
    inner[0] = jnp.where(alive, started[:, 0:L], 0.0).astype(BF)
    for i in (1, 3, 0, 2):
        copy, there, _ = inner_copies[i]

        @pl.when(there)
        def _(i=i, copy=copy):
            if i < 2:
                pl.semaphore_wait(near_sem.at[i], 1)
            copy.start()

    @pl.when(has_left)
    def _():
        to_right.wait_recv()

    @pl.when(has_right)
    def _():
        to_left.wait_recv()

    sides = jnp.where(lane < 80, halos[1].astype(F32), halos[0].astype(F32))
    xs[8:72, L:] = jnp.where(alive_halo, sides, 0.0)
    own = jnp.where((column * time_ok) > 0.0, filter_with(xs, 1, c1, started), 0.0)
    spare = (lane >= 64) & (lane < 96)
    outer[0] = jnp.where(spare, pltpu.roll(own[:, 0:L], L - 48, 1), own[:, L:]).astype(BF)
    for i in (1, 3, 0, 2):
        copy, there, _ = outer_copies[i]

        @pl.when(there)
        def _(copy=copy):
            copy.start()

    win[...] = own.astype(BF)

    lanes2 = iota((1, 2 * L), 1)

    def make_planes(offset, there):
        if offset == 0:
            values = win[...].astype(F32)
        else:
            slot = SLOT[offset]
            rim = outer[slot].astype(F32)
            middle = (lane >= 16) & (lane < 112)
            centre = jnp.where(middle, inner[slot].astype(F32), pltpu.roll(rim, 48, 1))
            values = jnp.where(there, jnp.concatenate([centre, rim], axis=1), 0.0)
        a = offset + SHOT_TAPS // 2
        planes[a] = pltpu.roll(values, GAP * a + 33, 1).astype(BF)
        p = a + SHOT_TAPS
        delay = dith[lax.rem(s + offset + shots, shots)]
        moved = pltpu.roll(values, GAP * p + 33 - delay, 1)
        early = (lanes2 >= GAP * p) & (lanes2 < GAP * p + 33)
        planes[p] = jnp.where(jnp.where(early, left_f, 1.0) > 0.0, moved, 0.0).astype(BF)

    same_half = (iota((L, L), 0) >= CH) == (iota((L, L), 1) >= CH)
    zero_block = jnp.zeros((L, L), BF)
    for layer in range(HID):
        weights = hw[layer]
        doubled = jnp.concatenate([weights, weights], axis=0)
        wh[layer, 3 * L :, 0:L] = zero_block
        wh[layer, 0:L, L:] = zero_block
        for k in range(3):
            pick = iota((L, 3 * CH), 1) == (k * CH + (iota((L, 3 * CH), 0) & (CH - 1)))
            block = jnp.where(same_half, dot_nt(pick.astype(BF), doubled), 0.0).astype(BF)
            wh[layer, k * L : (k + 1) * L, 0:L] = block
            wh[layer, (k + 1) * L : (k + 2) * L, L:] = block

    pick = iota((L, CH), 1) == (iota((L, CH), 0) & (CH - 1))
    spread = dot_nt(pick.astype(BF), jnp.broadcast_to(ow[...], (L, CH)))
    for r in range(4):
        for i in range(2):
            step = 8 * i + 2 * r
            here = (iota((L, L), 1) & 15) == step + jnp.where(iota((L, L), 0) >= CH, 1, 0)
            wo[(2 * r + i) * L : (2 * r + i + 1) * L, :] = jnp.where(here, spread, 0.0).astype(BF)

    def wide(bias):
        both = jnp.concatenate([bias, bias], axis=1)
        return jnp.concatenate([both, both], axis=1)

    first_bias = wide(fb[...])
    hidden_bias = [wide(hb[layer : layer + 1, :]) for layer in range(HID)]
    make_planes(0, None)

    def keep_second(a, near, far):
        c2[a, 0:L, :] = near
        c2[a, L:, :] = far

    circulants(shp[...], keep_second)
    def merge(numbers, begin, last):
        for part in range(2):
            rows = slice(part * 32, part * 32 + 32)
            held = {p: planes[p, rows, :] for p in numbers}
            for g in range(GROUPS):
                place = ((lanes2 - 16 * g) & 255).astype(F32).astype(BF)
                merged = held[numbers[0]] if begin else gs[g, rows, :]
                for p in numbers[1:] if begin else numbers:
                    inside = (place >= GAP * p) & (place < GAP * p + GAP)
                    merged = jnp.where(inside, held[p], merged)
                if last and g:
                    merged = pltpu.roll(merged.astype(F32), 256 - 16 * g, 1).astype(BF)
                gs[g, rows, :] = merged

    def arrived(i, offset):
        inside, _, behind = inner_copies[i]
        beyond = outer_copies[i][0]

        @pl.when(behind)
        def _():
            inside.wait_recv()
            beyond.wait_recv()
        make_planes(offset, behind)

    arrived(2, -1)
    arrived(3, 1)
    merge((1, 2, 3, 6, 7, 8), True, False)
    arrived(0, -2)
    arrived(1, 2)
    merge((0, 4, 5, 9), False, True)

    def finish(total, bias, factor):
        act = jnp.maximum(total + bias, 0.0)
        if factor is not None:
            act = act * factor
        return act.astype(BF)

    for g0, g1, factor in ((0, 2, left_f), (2, 6, None), (6, 10, None), (10, 12, right_f)):
        left = gs[g0:g1].reshape((g1 - g0) * N, 256)
        for quarter in range(4):
            act = finish(dot_nn(left, w0[:, quarter * 256 : (quarter + 1) * 256]), first_bias, factor)
            for g in range(g0, g1):
                for i in range(2):
                    at = (g - g0) * N
                    a0[8 * g + 2 * quarter + i] = act[at : at + N, i * L : (i + 1) * L]

    def chunks(lo, hi, size):
        cuts = [lo, 16 // size, 80 // size, hi]
        return [(cuts[0], cuts[1], left_f), (cuts[1], cuts[2], None), (cuts[2], cuts[3], right_f)]

    def layer(source, target, index, lo, hi, most):
        step = 1 << index
        for start, stop, factor in chunks(lo, hi, 2 * step):
            for j0 in range(start, stop, most):
                js = range(j0, min(j0 + most, stop))
                us = [2 * step * j + r for j in js for r in range(step)]
                left = jnp.concatenate(
                    [jnp.concatenate([source[u - step], source[u], source[u + step], source[u + 2 * step]], axis=1)
                     for u in us], axis=0)
                act = finish(dot_nn(left, wh[index]), hidden_bias[index], factor)
                target(us, step, act)

    def into(ref):
        def keep(us, step, act):
            for m, u in enumerate(us):
                ref[u] = act[m * N : (m + 1) * N, 0:L]
                ref[u + step] = act[m * N : (m + 1) * N, L:]
        return keep

    out_bias = ob[...]
    sixteen = lax.shift_right_logical(lane, 4)

    def last(us, step, act):
        for m, u in enumerate(us):
            r = m % step
            a3[u // 8 - 1, :, 2 * L * r : 2 * L * (r + 1)] = act[m * N : (m + 1) * N]

    layer(a0, into(a1), 0, 1, 47, 4)
    layer(a1, into(a2), 1, 1, 23, 2)
    layer(a2, last, 2, 1, 11, 1)
    scores = (dot_nn(a3[...].reshape(10 * N, 8 * L), wo[...]) + out_bias).astype(BF).astype(F32)
    pred = {j: scores[(j - 1) * N : j * N] for j in range(1, 11)}

    middle = pred[2]
    for j in range(3, 10):
        middle = jnp.where(sixteen == j - 2, pred[j], middle)
    middle = jnp.where(alive, middle, 0.0)
    out[0] = middle.astype(BF)
    edge = jnp.where(lane < 80, pred[10], pred[1])
    edge = jnp.where(alive_halo, edge, 0.0)
    rest = (win[...].astype(F32) - jnp.concatenate([middle, edge], axis=1)).astype(BF).astype(F32)
    ds[0:8, :] = jnp.zeros((8, 2 * L), F32)
    ds[72:80, :] = jnp.zeros((8, 2 * L), F32)
    ds[8:72, :] = rest
    out[1] = jnp.where(alive, filter_with(ds, None, c2), 0.0).astype(BF)

    for here, copy in (
        (has_right, to_right),
        (has_left, to_left),
        *[(there, copy) for copy, there, _ in inner_copies + outer_copies],
    ):
        @pl.when(here)
        def _(copy=copy):
            copy.wait_send()


def local(shots, tms, records, live, dither, designature, first_weights, first_bias, hidden_weights, hidden_bias,
          out_weights, out_bias, shaping):
    vmem = pl.BlockSpec(memory_space=pltpu.VMEM)
    hbm = pl.BlockSpec(memory_space=pltpu.HBM)
    shape = pltpu.VMEM((2, N, L), BF)
    inputs = (
        records.reshape(N, L),
        live,
        dither,
        designature,
        first_weights.T,
        first_bias.reshape(1, CH),
        hidden_weights,
        hidden_bias,
        out_weights.reshape(1, CH),
        out_bias.reshape(1, 1),
        shaping,
    )
    spaces = [pltpu.SMEM if i == 2 else pltpu.VMEM for i in range(len(inputs))]
    both = pl.pallas_call(
        functools.partial(kernel, shots, tms),
        out_shape=shape,
        in_specs=[hbm] * len(inputs),
        out_specs=vmem,
        scratch_shapes=[
            *[space(x.shape, x.dtype) for space, x in zip(spaces, inputs)],
            pltpu.VMEM((2, N, L), BF),
            pltpu.VMEM((5, N, L), BF),
            pltpu.VMEM((5, N, L), BF),
            pltpu.VMEM((N, 2 * L), BF),
            pltpu.VMEM((80, 2 * L), F32),
            pltpu.VMEM((FN, 2 * L, 2 * L), BF),
            pltpu.VMEM((FN, 2 * L, L), BF),
            pltpu.VMEM((256, 1024), BF),
            pltpu.VMEM((HID, 4 * L, 2 * L), BF),
            pltpu.VMEM((1024, L), BF),
            pltpu.VMEM((272, L), F32),
            pltpu.VMEM((2 * SHOT_TAPS, N, 2 * L), BF),
            pltpu.VMEM((GROUPS, N, 2 * L), BF),
            pltpu.VMEM((US, N, L), BF),
            pltpu.VMEM((US, N, L), BF),
            pltpu.VMEM((US, N, L), BF),
            pltpu.VMEM((10, N, 8 * L), BF),
            pltpu.VMEM((80, 2 * L), F32),
            pltpu.SemaphoreType.DMA((len(inputs),)),
            pltpu.SemaphoreType.DMA((2,)),
            pltpu.SemaphoreType.DMA((2,)),
            pltpu.SemaphoreType.DMA((8,)),
            pltpu.SemaphoreType.DMA((8,)),
            pltpu.SemaphoreType.REGULAR((2,)),
        ],
        compiler_params=pltpu.CompilerParams(
            collective_id=0, has_side_effects=True, vmem_limit_bytes=61 * 1024 * 1024
        ),
    )(*inputs)
    return both[0:1], both[1:2]


def solution(mesh):
    shots, tms = mesh.shape["shot"], mesh.shape["tm"]
    in_specs = (P("shot", None, "tm"), P("shot", None), P(), P(), P(), P(), P(), P(), P(), P(), P())
    out_specs = (P("shot", None, "tm"), P("shot", None, "tm"))
    return jax.shard_map(
        functools.partial(local, shots, tms), mesh=mesh, in_specs=in_specs, out_specs=out_specs, check_vma=False
    )
```

```python
import functools

import jax
import jax.numpy as jnp
from jax import lax
from jax.experimental import pallas as pl
from jax.experimental.pallas import tpu as pltpu
from jax.sharding import PartitionSpec as P

HID = 3
FN = 9
FT = 33
SHOT_TAPS = 5
CH = 64
N = 64
L = 128
GAP = 24
GROUPS = 12
US = 8 * GROUPS
SLOT = {0: 0, -1: 1, 1: 2, -2: 3, 2: 4}
MESH = pl.DeviceIdType.MESH
BF = jnp.bfloat16
F32 = jnp.float32


def iota(shape, dim):
    return lax.broadcasted_iota(jnp.int32, shape, dim)


def dot_nn(a, b):
    return jnp.dot(a, b, preferred_element_type=F32)


def dot_nt(a, b):
    return lax.dot_general(a, b, (((1,), (1,)), ((), ())), preferred_element_type=F32)


def circulants(taps, store):
    pick = iota((FT, L), 0) == ((FT // 2 - iota((FT, L), 1)) & (L - 1))
    rows = dot_nn(taps, pick.astype(BF))
    near = jnp.abs(iota((L, L), 0) - iota((L, L), 1)) <= L // 2
    for a in range(FN):
        full = jnp.broadcast_to(rows[a : a + 1, :], (L, L))
        full = pltpu.roll(full, 0, 1, stride=1, stride_axis=0)
        store(a, jnp.where(near, full, 0.0).astype(BF), jnp.where(near, 0.0, full).astype(BF))


def kernel(
    shots,
    tms,
    rec_hbm,
    live_hbm,
    dith_hbm,
    des_hbm,
    fw_hbm,
    fb_hbm,
    hw_hbm,
    hb_hbm,
    ow_hbm,
    ob_hbm,
    shp_hbm,
    out,
    rec,
    live,
    dith,
    des,
    fw,
    fb,
    hw,
    hb,
    ow,
    ob,
    shp,
    halos,
    win,
    xs,
    c1,
    c2,
    w0,
    wh,
    wo,
    b0s,
    planes,
    gs,
    a0,
    a1,
    a2,
    a3,
    ds,
    in_sem,
    tm_send,
    tm_recv,
    shot_send,
    shot_recv,
    near_sem,
):
    s, z = lax.axis_index("shot"), lax.axis_index("tm")
    has_left, has_right = z > 0, z < tms - 1
    has_before, has_after = s > 0, s < shots - 1
    has_before2, has_after2 = s > 1, s < shots - 2

    barrier = pltpu.get_barrier_semaphore()
    expected = 0
    for here, device in (
        (has_left, (s, z - 1)),
        (has_right, (s, z + 1)),
        (has_before, (s - 1, z)),
        (has_after, (s + 1, z)),
    ):
        @pl.when(here)
        def _(device=device):
            pl.semaphore_signal(barrier, inc=1, device_id=device, device_id_type=MESH)
        expected = expected + here.astype(jnp.int32)

    fetches = [
        pltpu.make_async_copy(src, dst, in_sem.at[i])
        for i, (src, dst) in enumerate((
            (des_hbm, des), (rec_hbm, rec), (live_hbm, live), (fw_hbm, fw), (hw_hbm, hw), (dith_hbm, dith),
            (ow_hbm, ow), (shp_hbm, shp), (fb_hbm, fb), (hb_hbm, hb), (ob_hbm, ob)))
    ]
    for fetch in fetches:
        fetch.start()

    def remote(src, dst, send_sem, recv_sem, device):
        return pltpu.make_async_remote_copy(
            src_ref=src, dst_ref=dst, send_sem=send_sem, recv_sem=recv_sem,
            device_id=device, device_id_type=MESH,
        )

    to_right = remote(rec_hbm, halos.at[0], tm_send.at[0], tm_recv.at[0], (s, z + 1))
    to_left = remote(rec_hbm, halos.at[1], tm_send.at[1], tm_recv.at[1], (s, z - 1))

    def to_shot(index, offset):
        return remote(
            win.at[0], win.at[SLOT[-offset]], shot_send.at[index], shot_recv.at[index], (s + offset, z))

    shot_copies = [
        (to_shot(i, offset), there, behind)
        for i, (offset, there, behind) in enumerate((
            (2, has_after2, has_before2),
            (-2, has_before2, has_after2),
            (1, has_after, has_before),
            (-1, has_before, has_after)))
    ]

    def keep_first(a, near, far):
        c1[a, 0:L, 0:L] = near
        c1[a, 0:L, L:] = far
        c1[a, L:, 0:L] = far
        c1[a, L:, L:] = near

    pl.semaphore_wait(barrier, expected)

    @pl.when(has_left)
    def _():
        to_left.start()

    @pl.when(has_right)
    def _():
        to_right.start()

    @pl.when(has_before & has_after)
    def _():
        pl.semaphore_signal(near_sem.at[0], inc=1, device_id=(s - 1, z), device_id_type=MESH)
        pl.semaphore_signal(near_sem.at[1], inc=1, device_id=(s + 1, z), device_id_type=MESH)

    for fetch in fetches:
        fetch.wait()
    circulants(des[...], keep_first)

    lane = iota((1, L), 1)
    left_f, right_f = jnp.where(has_left, 1.0, 0.0), jnp.where(has_right, 1.0, 0.0)
    halo = jnp.where(lane < 80, right_f, left_f)
    time_ok = jnp.concatenate([jnp.ones((1, L), F32), halo], axis=1)
    diagonal = iota((N, N), 0) == iota((N, N), 1)
    spread_rows = jnp.where(diagonal, jnp.broadcast_to(live[...].astype(F32), (N, N)), 0.0)
    column = jnp.sum(spread_rows, axis=1, keepdims=True)
    alive = column > 0.0
    alive_halo = (column * halo) > 0.0

    xs[0:8, :] = jnp.zeros((8, 2 * L), F32)
    xs[72:80, :] = jnp.zeros((8, 2 * L), F32)
    xs[8:72, 0:L] = jnp.where(alive, rec[...].astype(F32), 0.0)

    upper = lane >= CH
    row, col = iota((256, 6 * SHOT_TAPS), 0), iota((256, 6 * SHOT_TAPS), 1)
    third = lax.shift_right_logical(col * 43, 7)
    place = row == GAP * third + (col - 3 * third)
    base = dot_nn(place.astype(BF), fw[...])
    b0s[0:16, :] = jnp.zeros((16, L), F32)
    b0s[16:, :] = jnp.concatenate([base, base], axis=1)
    for pair in range(8):
        even, odd = b0s[pl.ds(16 - 2 * pair, 256), :], b0s[pl.ds(15 - 2 * pair, 256), :]
        w0[:, pair * L : (pair + 1) * L] = jnp.where(upper, odd, even).astype(BF)

    @pl.when(has_left)
    def _():
        to_right.wait_recv()

    @pl.when(has_right)
    def _():
        to_left.wait_recv()

    sides = jnp.where(lane < 80, halos[1].astype(F32), halos[0].astype(F32))
    xs[8:72, L:] = jnp.where(alive_halo, sides, 0.0)

    def filter_with(source, matrices):
        total = None
        for a in range(FN):
            term = dot_nn(source[pl.ds(4 + a, N), :].astype(BF), matrices[a])
            total = term if total is None else total + term
        return total

    win[0] = jnp.where((column * time_ok) > 0.0, filter_with(xs, c1), 0.0).astype(BF)

    for i in (1, 3, 0, 2):
        copy, there, _ = shot_copies[i]

        @pl.when(there)
        def _(i=i, copy=copy):
            if i < 2:
                pl.semaphore_wait(near_sem.at[i], 1)
            copy.start()

    lanes2 = iota((1, 2 * L), 1)

    def make_planes(offset, there):
        values = win[SLOT[offset]].astype(F32)
        if there is not None:
            values = jnp.where(there, values, 0.0)
        a = offset + SHOT_TAPS // 2
        planes[a] = pltpu.roll(values, GAP * a + 33, 1).astype(BF)
        p = a + SHOT_TAPS
        delay = dith[lax.rem(s + offset + shots, shots)]
        moved = pltpu.roll(values, GAP * p + 33 - delay, 1)
        early = (lanes2 >= GAP * p) & (lanes2 < GAP * p + 33)
        planes[p] = jnp.where(jnp.where(early, left_f, 1.0) > 0.0, moved, 0.0).astype(BF)

    same_half = (iota((L, L), 0) >= CH) == (iota((L, L), 1) >= CH)
    zero_block = jnp.zeros((L, L), BF)
    for layer in range(HID):
        weights = hw[layer]
        doubled = jnp.concatenate([weights, weights], axis=0)
        wh[layer, 3 * L :, 0:L] = zero_block
        wh[layer, 0:L, L:] = zero_block
        for k in range(3):
            pick = iota((L, 3 * CH), 1) == (k * CH + (iota((L, 3 * CH), 0) & (CH - 1)))
            block = jnp.where(same_half, dot_nt(pick.astype(BF), doubled), 0.0).astype(BF)
            wh[layer, k * L : (k + 1) * L, 0:L] = block
            wh[layer, (k + 1) * L : (k + 2) * L, L:] = block

    pick = iota((L, CH), 1) == (iota((L, CH), 0) & (CH - 1))
    spread = dot_nt(pick.astype(BF), jnp.broadcast_to(ow[...], (L, CH)))
    for r in range(4):
        for i in range(2):
            step = 8 * i + 2 * r
            here = (iota((L, L), 1) & 15) == step + jnp.where(iota((L, L), 0) >= CH, 1, 0)
            wo[(2 * r + i) * L : (2 * r + i + 1) * L, :] = jnp.where(here, spread, 0.0).astype(BF)

    def wide(bias):
        both = jnp.concatenate([bias, bias], axis=1)
        return jnp.concatenate([both, both], axis=1)

    first_bias = wide(fb[...])
    hidden_bias = [wide(hb[layer : layer + 1, :]) for layer in range(HID)]
    make_planes(0, None)

    def keep_second(a, near, far):
        c2[a, 0:L, :] = near
        c2[a, L:, :] = far

    circulants(shp[...], keep_second)
    def merge(numbers, begin, last):
        for part in range(2):
            rows = slice(part * 32, part * 32 + 32)
            held = {p: planes[p, rows, :] for p in numbers}
            for g in range(GROUPS):
                place = ((lanes2 - 16 * g) & 255).astype(F32).astype(BF)
                merged = held[numbers[0]] if begin else gs[g, rows, :]
                for p in numbers[1:] if begin else numbers:
                    inside = (place >= GAP * p) & (place < GAP * p + GAP)
                    merged = jnp.where(inside, held[p], merged)
                if last and g:
                    merged = pltpu.roll(merged.astype(F32), 256 - 16 * g, 1).astype(BF)
                gs[g, rows, :] = merged

    for i, offset in ((2, -1), (3, 1), (0, -2), (1, 2)):
        copy, _, behind = shot_copies[i]

        @pl.when(behind)
        def _(copy=copy):
            copy.wait_recv()
        make_planes(offset, behind)
        if offset == 1:
            merge((1, 2, 3, 6, 7, 8), True, False)

    merge((0, 4, 5, 9), False, True)

    def finish(total, bias, factor):
        act = jnp.maximum(total + bias, 0.0)
        if factor is not None:
            act = act * factor
        return act.astype(BF)

    for g0, g1, factor in ((0, 2, left_f), (2, 6, None), (6, 10, None), (10, 12, right_f)):
        left = gs[g0:g1].reshape((g1 - g0) * N, 256)
        for quarter in range(4):
            act = finish(dot_nn(left, w0[:, quarter * 256 : (quarter + 1) * 256]), first_bias, factor)
            for g in range(g0, g1):
                for i in range(2):
                    at = (g - g0) * N
                    a0[8 * g + 2 * quarter + i] = act[at : at + N, i * L : (i + 1) * L]

    def chunks(lo, hi, size):
        cuts = [lo, 16 // size, 80 // size, hi]
        return [(cuts[0], cuts[1], left_f), (cuts[1], cuts[2], None), (cuts[2], cuts[3], right_f)]

    def layer(source, target, index, lo, hi, most):
        step = 1 << index
        for start, stop, factor in chunks(lo, hi, 2 * step):
            for j0 in range(start, stop, most):
                js = range(j0, min(j0 + most, stop))
                us = [2 * step * j + r for j in js for r in range(step)]
                left = jnp.concatenate(
                    [jnp.concatenate([source[u - step], source[u], source[u + step], source[u + 2 * step]], axis=1)
                     for u in us], axis=0)
                act = finish(dot_nn(left, wh[index]), hidden_bias[index], factor)
                target(us, step, act)

    def into(ref):
        def keep(us, step, act):
            for m, u in enumerate(us):
                ref[u] = act[m * N : (m + 1) * N, 0:L]
                ref[u + step] = act[m * N : (m + 1) * N, L:]
        return keep

    out_bias = ob[...]
    sixteen = lax.shift_right_logical(lane, 4)

    def last(us, step, act):
        for m, u in enumerate(us):
            r = m % step
            a3[u // 8 - 1, :, 2 * L * r : 2 * L * (r + 1)] = act[m * N : (m + 1) * N]

    layer(a0, into(a1), 0, 1, 47, 4)
    layer(a1, into(a2), 1, 1, 23, 2)
    layer(a2, last, 2, 1, 11, 1)
    scores = (dot_nn(a3[...].reshape(10 * N, 8 * L), wo[...]) + out_bias).astype(BF).astype(F32)
    pred = {j: scores[(j - 1) * N : j * N] for j in range(1, 11)}

    middle = pred[2]
    for j in range(3, 10):
        middle = jnp.where(sixteen == j - 2, pred[j], middle)
    middle = jnp.where(alive, middle, 0.0)
    out[0] = middle.astype(BF)
    edge = jnp.where(lane < 80, pred[10], pred[1])
    edge = jnp.where(alive_halo, edge, 0.0)
    rest = (win[0].astype(F32) - jnp.concatenate([middle, edge], axis=1)).astype(BF).astype(F32)
    ds[0:8, :] = jnp.zeros((8, 2 * L), F32)
    ds[72:80, :] = jnp.zeros((8, 2 * L), F32)
    ds[8:72, :] = rest
    out[1] = jnp.where(alive, filter_with(ds, c2), 0.0).astype(BF)

    for here, copy in (
        (has_right, to_right),
        (has_left, to_left),
        *[(there, copy) for copy, there, _ in shot_copies],
    ):
        @pl.when(here)
        def _(copy=copy):
            copy.wait_send()


def local(shots, tms, records, live, dither, designature, first_weights, first_bias, hidden_weights, hidden_bias,
          out_weights, out_bias, shaping):
    vmem = pl.BlockSpec(memory_space=pltpu.VMEM)
    hbm = pl.BlockSpec(memory_space=pltpu.HBM)
    shape = pltpu.VMEM((2, N, L), BF)
    inputs = (
        records.reshape(N, L),
        live,
        dither,
        designature,
        first_weights.T,
        first_bias.reshape(1, CH),
        hidden_weights,
        hidden_bias,
        out_weights.reshape(1, CH),
        out_bias.reshape(1, 1),
        shaping,
    )
    spaces = [pltpu.SMEM if i == 2 else pltpu.VMEM for i in range(len(inputs))]
    both = pl.pallas_call(
        functools.partial(kernel, shots, tms),
        out_shape=shape,
        in_specs=[hbm] * len(inputs),
        out_specs=vmem,
        scratch_shapes=[
            *[space(x.shape, x.dtype) for space, x in zip(spaces, inputs)],
            pltpu.VMEM((2, N, L), BF),
            pltpu.VMEM((5, N, 2 * L), BF),
            pltpu.VMEM((80, 2 * L), F32),
            pltpu.VMEM((FN, 2 * L, 2 * L), BF),
            pltpu.VMEM((FN, 2 * L, L), BF),
            pltpu.VMEM((256, 1024), BF),
            pltpu.VMEM((HID, 4 * L, 2 * L), BF),
            pltpu.VMEM((1024, L), BF),
            pltpu.VMEM((272, L), F32),
            pltpu.VMEM((2 * SHOT_TAPS, N, 2 * L), BF),
            pltpu.VMEM((GROUPS, N, 2 * L), BF),
            pltpu.VMEM((US, N, L), BF),
            pltpu.VMEM((US, N, L), BF),
            pltpu.VMEM((US, N, L), BF),
            pltpu.VMEM((10, N, 8 * L), BF),
            pltpu.VMEM((80, 2 * L), F32),
            pltpu.SemaphoreType.DMA((len(inputs),)),
            pltpu.SemaphoreType.DMA((2,)),
            pltpu.SemaphoreType.DMA((2,)),
            pltpu.SemaphoreType.DMA((4,)),
            pltpu.SemaphoreType.DMA((4,)),
            pltpu.SemaphoreType.REGULAR((2,)),
        ],
        compiler_params=pltpu.CompilerParams(
            collective_id=0, has_side_effects=True, vmem_limit_bytes=61 * 1024 * 1024
        ),
    )(*inputs)
    return both[0:1], both[1:2]


def solution(mesh):
    shots, tms = mesh.shape["shot"], mesh.shape["tm"]
    in_specs = (P("shot", None, "tm"), P("shot", None), P(), P(), P(), P(), P(), P(), P(), P(), P())
    out_specs = (P("shot", None, "tm"), P("shot", None, "tm"))
    return jax.shard_map(
        functools.partial(local, shots, tms), mesh=mesh, in_specs=in_specs, out_specs=out_specs, check_vma=False
    )
```
